512 devices in a mesh: leaf: 512 (over y, x, z, core).
Axes of the slice: x: 4, y: 4, z: 16, core: 2. Of those that a mesh axis runs over, the one named last changes fastest.
Arguments:
- densities: float32 [16, 524288], P(None, 'leaf'), may hold values from -6 to 6
- points: float32 [3, 524288], P(None, 'leaf'), may hold values from 0 to 1
- area_normals: float32 [3, 524288], P(None, 'leaf'), may hold values from -0.234375 to 0.234375
- col_basis: float32 [64, 524288], P(None, 'leaf'), may hold values from -0.375 to 0.375
- row_basis: float32 [64, 524288], P(None, 'leaf'), may hold values from -0.75 to 0.75
- up_leaf: float32 [2048, 4096], P('leaf'), may hold values from -0.5 to 0.5
- up_mid: float32 [1024, 4096], P('leaf'), may hold values from -0.5 to 0.5
- down_leaf: float32 [2048, 4096], P('leaf'), may hold values from -0.5 to 0.5
- down_mid: float32 [1024, 4096], P('leaf'), may hold values from -0.5 to 0.5
- couple_leaf: float32 [2048, 6, 4096], P('leaf'), may hold values from -0.3125 to 0.3125
- couple_mid: float32 [1024, 6, 4096], P('leaf'), may hold values from -0.3125 to 0.3125
- couple_top: float32 [512, 16, 4096], P('leaf'), may hold values from -0.1875 to 0.1875
- near_list: int32 [2048, 8], P('leaf'), may hold values from 0 to 2047, as said below
- near_count: int32 [2048], P('leaf'), may hold values from 1 to 8
- adm_leaf: int32 [2048, 6], P('leaf'), may hold values from 0 to 2047, as said below
- adm_mid: int32 [1024, 6], P('leaf'), may hold values from 0 to 1023, as said below
- adm_top: int32 [512, 16], P('leaf'), may hold values from 0 to 511
Outputs:
- potential: float32 [16, 524288], P(None, 'leaf')
The draws below stay inside these ranges and needn't reach their ends.
Inputs may be any that keep to these rules, and one draw needn't show every extreme that they name: `near_list`: entry 0 of each row is the leaf itself; every other entry lies within 4 leaves of it. `adm_leaf`: every source lies in the leaf range of the device just before or just after the one that holds the target leaf. `adm_mid`: every source lies among the middle-level clusters of the device just before or just after the one that holds the target.
All inputs are finite; a program needn't handle non-finite values.
Results may differ from the reference program's by a relative error of at most 0.0003.
Values sent between devices are 32-bit elements; how exact they have to be, the bound alone decides.
No kernel may reach another device: no remote copies, remote signals or barrier semaphores. Data moves between devices by JAX's collectives and lax.ppermute only.
A program may use at most 64 MiB of HBM per device.

```python
import math
import jax
import jax.numpy as jnp
from jax import lax

RHS = 16
LEAF = 256
RANK = 64
LEAF_DEV = 4
NEAR = 8
ADM_LEAF = 6
ADM_MID = 6
ADM_TOP = 16
LEAVES = 2048
MIDS = 1024
TOPS = 512
POINTS = 524288
N_LEAF = 512


def neighbour_lists(key, clusters, per_device, slots):
    cluster_ids = jnp.arange(clusters, dtype=jnp.int32)[:, None]
    owner = cluster_ids // per_device
    sides = jnp.where(jnp.arange(slots, dtype=jnp.int32) % 2 == 0, 1, -1)[None, :]
    ahead = owner + sides
    behind = owner - sides
    source_dev = jnp.where((ahead >= 0) & (ahead < N_LEAF), ahead, behind)
    within = jax.random.randint(key, (clusters, slots), 0, per_device)
    return (source_dev * per_device + within).astype(jnp.int32)


def draw_near_list(key, part):
    key = jax.random.fold_in(key, 11)
    leaf_ids = jnp.arange(LEAVES, dtype=jnp.int32)[:, None]
    offsets = jax.random.randint(key, (LEAVES, NEAR), 1, LEAF_DEV + 1)
    signs = jnp.where(jnp.arange(NEAR, dtype=jnp.int32) % 2 == 0, 1, -1)[None, :]
    ahead = leaf_ids + signs * offsets
    behind = leaf_ids - signs * offsets
    chosen = jnp.where((ahead >= 0) & (ahead < LEAVES), ahead, behind)
    first_slot = jnp.arange(NEAR, dtype=jnp.int32)[None, :] == 0
    chosen = jnp.where(first_slot, leaf_ids, chosen)
    return chosen.astype(jnp.int32)


def draw_near_count(key, part):
    key = jax.random.fold_in(key, 23)
    counts = jax.random.randint(key, (LEAVES,), 1, NEAR + 1)
    leaf_ids = jnp.arange(LEAVES, dtype=jnp.int32)
    return jnp.where(leaf_ids % 5 == 0, NEAR, counts).astype(jnp.int32)


def draw_adm_leaf(key, part):
    key = jax.random.fold_in(key, 37)
    return neighbour_lists(key, LEAVES, LEAF_DEV, ADM_LEAF)


def draw_adm_mid(key, part):
    key = jax.random.fold_in(key, 41)
    return neighbour_lists(key, MIDS, LEAF_DEV // 2, ADM_MID)


def with_ends(drawn, own_key, low, largest):
    spot = [jax.random.randint(jax.random.fold_in(own_key, axis), (), 0, length) for axis, length in enumerate(drawn.shape)]
    widest = drawn.shape.index(max(drawn.shape))
    neighbour = spot[:widest] + [(spot[widest] + 1) % drawn.shape[widest]] + spot[widest + 1:]
    return drawn.at[tuple(spot)].set(low).at[tuple(neighbour)].set(largest)


def block_scale(own_key, shape, split, smallest, largest):
    loudness = 1.0
    for position, parts in split:
        draws = jax.random.uniform(jax.random.fold_in(jax.random.fold_in(own_key, 6), position), (parts,), jnp.float32, smallest / len(split), largest / len(split))
        loudness = loudness * jnp.repeat(jnp.exp(draws), shape[position] // parts).reshape((-1,) + (1,) * (len(shape) - 1 - position))
    return loudness


def normal_values(stream_key, extent, width, limit, pieces=(), held_as=jnp.bfloat16):
    result = width * jax.random.normal(stream_key, extent, jnp.float32)
    if pieces:
        result = result * block_scale(stream_key, extent, pieces, -0.22, 0.18)
    return jnp.clip(result, -limit, limit).astype(held_as)


def setup_inputs(seed: int = 0) -> dict:
    splits = jax.random.split(jax.random.key(seed), 18)
    return {
        "densities": normal_values(splits[0], (RHS, POINTS), 1.0, 6.0, ((1, 512),), jnp.float32),
        "points": jnp.clip(1.0 * jax.random.uniform(splits[1], (3, POINTS), jnp.float32) ** block_scale(splits[1], (3, POINTS), ((1, 512),), -0.2, 0.2), 0.0, 1.0),
        "area_normals": normal_values(splits[2], (3, POINTS), (10.0 / LEAF), 0.234375, ((1, 512),), jnp.float32),
        "col_basis": normal_values(splits[3], (RANK, POINTS), LEAF ** -0.5, 0.375, ((1, 512),), jnp.float32),
        "row_basis": normal_values(splits[4], (RANK, POINTS), RANK ** -0.5, 0.75, ((1, 512),), jnp.float32),
        "up_leaf": normal_values(splits[5], (LEAVES, RANK * RANK), (2 * RANK) ** -0.5, 0.5, ((0, 512),), jnp.float32),
        "up_mid": normal_values(splits[6], (MIDS, RANK * RANK), (2 * RANK) ** -0.5, 0.5, ((0, 512),), jnp.float32),
        "down_leaf": normal_values(splits[7], (LEAVES, RANK * RANK), (2 * RANK) ** -0.5, 0.5, ((0, 512),), jnp.float32),
        "down_mid": normal_values(splits[8], (MIDS, RANK * RANK), (2 * RANK) ** -0.5, 0.5, ((0, 512),), jnp.float32),
        "couple_leaf": normal_values(splits[9], (LEAVES, ADM_LEAF, RANK * RANK), (ADM_LEAF * RANK) ** -0.5, 0.3125, ((0, 512),), jnp.float32),
        "couple_mid": normal_values(splits[10], (MIDS, ADM_MID, RANK * RANK), (ADM_MID * RANK) ** -0.5, 0.3125, ((0, 512),), jnp.float32),
        "couple_top": normal_values(splits[11], (TOPS, ADM_TOP, RANK * RANK), (ADM_TOP * RANK) ** -0.5, 0.1875, ((0, 512),), jnp.float32),
        "near_list": draw_near_list(jax.random.fold_in(splits[17], 71), 0),
        "near_count": draw_near_count(jax.random.fold_in(splits[17], 71), 0),
        "adm_leaf": draw_adm_leaf(jax.random.fold_in(splits[17], 71), 0),
        "adm_mid": draw_adm_mid(jax.random.fold_in(splits[17], 71), 0),
        "adm_top": with_ends(jax.random.randint(splits[16], (TOPS, ADM_TOP), 0, TOPS), jax.random.fold_in(splits[16], 1), 0, TOPS - 1).astype(jnp.int32),
    }


smooth_sq = 0.01
four_pi = 4.0 * math.pi
highest = lax.Precision.HIGHEST

def kernel_block(target, source, normals):
    delta_x = target[0][None, :] - source[0][:, None]
    delta_y = target[1][None, :] - source[1][:, None]
    delta_z = target[2][None, :] - source[2][:, None]
    radius_sq = delta_x * delta_x + delta_y * delta_y + delta_z * delta_z + smooth_sq
    along = normals[0][:, None] * delta_x + normals[1][:, None] * delta_y + normals[2][:, None] * delta_z
    return along / (four_pi * radius_sq * jnp.sqrt(radius_sq))

def coefficients(dens_rows, basis_rows, cluster_count):
    return jnp.einsum('rlp,klp->lrk', dens_rows.reshape(RHS, cluster_count, LEAF), basis_rows.reshape(RANK, cluster_count, LEAF), precision=highest)

def climb(children, transfers):
    groups = transfers.shape[0]
    return jnp.einsum('mcrk,mckj->mrj', children.reshape(groups, 2, RHS, RANK), transfers, precision=highest)

def descend(parents, transfers, coupled):
    groups = parents.shape[0]
    total = coupled.reshape(groups, 2, RHS, RANK) + jnp.einsum('mrk,mckj->mcrj', parents, transfers, precision=highest)
    return total.reshape(groups * 2, RHS, RANK)

def couple(sources, blocks):
    return jnp.einsum('tark,takj->trj', sources, blocks, precision=highest)

def near_field(densities, points, area_normals, near_list, near_count):

    def one_leaf(item):
        leaf_id, sources, count = item
        target = lax.dynamic_slice_in_dim(points, leaf_id * LEAF, LEAF, 1)
        total = jnp.zeros((RHS, LEAF), jnp.float32)
        for slot_index in range(NEAR):
            start = (sources[slot_index] * LEAF).astype(jnp.int32)
            block = kernel_block(target, lax.dynamic_slice_in_dim(points, start, LEAF, 1), lax.dynamic_slice_in_dim(area_normals, start, LEAF, 1))
            term = jnp.dot(lax.dynamic_slice_in_dim(densities, start, LEAF, 1), block, precision=highest)
            total = total + jnp.where(slot_index < count, term, jnp.zeros_like(term))
        return total
    blocks = lax.map(one_leaf, (jnp.arange(LEAVES, dtype=jnp.int32), near_list, near_count))
    return jnp.transpose(blocks, (1, 0, 2)).reshape(RHS, POINTS)

def reference(densities, points, area_normals, col_basis, row_basis, up_leaf, up_mid, down_leaf, down_mid, couple_leaf, couple_mid, couple_top, near_list, near_count, adm_leaf, adm_mid, adm_top):
    near_part = near_field(densities, points, area_normals, near_list, near_count)
    leaf_coef = coefficients(densities, col_basis, LEAVES)
    mid_coef = climb(leaf_coef, up_leaf.reshape(MIDS, 2, RANK, RANK))
    top_coef = climb(mid_coef, up_mid.reshape(TOPS, 2, RANK, RANK))
    top_field = couple(top_coef[adm_top], couple_top.reshape(TOPS, ADM_TOP, RANK, RANK))
    mid_couple = couple(mid_coef[adm_mid], couple_mid.reshape(MIDS, ADM_MID, RANK, RANK))
    mid_field = descend(top_field, down_mid.reshape(TOPS, 2, RANK, RANK), mid_couple)
    leaf_couple = couple(leaf_coef[adm_leaf], couple_leaf.reshape(LEAVES, ADM_LEAF, RANK, RANK))
    leaf_field = descend(mid_field, down_leaf.reshape(MIDS, 2, RANK, RANK), leaf_couple)
    far_part = jnp.einsum('lrk,klp->rlp', leaf_field, row_basis.reshape(RANK, LEAVES, LEAF), precision=highest).reshape(RHS, POINTS)
    return 0.5 * densities + near_part + far_part
```

```python
import math

import jax
import jax.numpy as jnp
from jax import lax
from jax.experimental import pallas as pl
from jax.experimental.pallas import tpu as pltpu
from jax.sharding import PartitionSpec as P

RHS = 16
LEAF = 256
RANK = 64
HALF = RANK // 2
LEAF_DEV = 4
MID_DEV = 2
NEAR = 8
ADM_LEAF = 6
ADM_MID = 6
ADM_TOP = 16
SPAN = LEAF_DEV * LEAF
CHUNKS = RANK * RANK // 128
FEATURES = 32
PACKED_ROWS = 32
COEF_ROW = 24

smooth_sq = 0.01
four_pi = 4.0 * math.pi
highest = lax.Precision.HIGHEST
f32 = jnp.float32
bf16 = jnp.bfloat16

SMEM = pl.BlockSpec(memory_space=pltpu.SMEM)
VMEM = pl.BlockSpec(memory_space=pltpu.VMEM)
ANY = pl.BlockSpec(memory_space=pl.ANY)


def dot(lhs, rhs, lhs_dim=1, rhs_dim=0):
    return lax.dot_general(
        lhs,
        rhs,
        (((lhs_dim,), (rhs_dim,)), ((), ())),
        precision=highest,
        preferred_element_type=f32,
    )


def even_odd(ref, index):
    even = ref[index, pl.ds(0, HALF, stride=2), :]
    odd = ref[index, pl.ds(1, HALF, stride=2), :]
    return jnp.concatenate([even[:, :RHS], odd[:, :RHS]], axis=1)


def pack(split):
    return jnp.concatenate([split[8 * g : 8 * g + 8] for g in range(4)], axis=1)


def unpack(tile):
    return jnp.concatenate([tile[:, 32 * g : 32 * g + 32] for g in range(4)], axis=0)


def fold(product):
    return product[:RANK, :RHS] + product[RANK:, RHS:]


def up_kernel(dens, points, normals, col_basis, up_leaf, up_mid, top_out, packed, leaf_rows, mid_rows, leaf_t, mid_t):
    packed[0:RHS, :] = dens[...]
    packed[RHS : RHS + 3, :] = points[...]
    packed[RHS + 3 : RHS + 6, :] = normals[...]
    packed[RHS + 6 : COEF_ROW, :] = jnp.zeros((COEF_ROW - RHS - 6, SPAN), f32)
    packed[COEF_ROW:, 6 * 128 :] = jnp.zeros((8, SPAN - 6 * 128), f32)
    for chunk in range(CHUNKS):
        lanes = slice(128 * chunk, 128 * chunk + 128)
        leaf_rows[8 * chunk : 8 * chunk + LEAF_DEV, :] = up_leaf[:, lanes]
        mid_rows[8 * chunk : 8 * chunk + MID_DEV, :] = up_mid[:, lanes]
    for c in range(LEAF_DEV):
        cols = slice(LEAF * c, LEAF * c + LEAF)
        leaf_t[c, :, 0:RHS] = dot(col_basis[:, cols], dens[:, cols], 1, 1)
    leaf_split = [even_odd(leaf_t, c) for c in range(LEAF_DEV)]
    for c in range(LEAF_DEV):
        packed[COEF_ROW:, 128 * c : 128 * c + 128] = pack(leaf_split[c])
    for m in range(MID_DEV):
        pair = (2 * m, 2 * m + 1)
        lhs = jnp.concatenate([leaf_rows[pl.ds(c, CHUNKS, stride=8), :] for c in pair], axis=0)
        rhs = jnp.concatenate([leaf_split[c] for c in pair], axis=0)
        mid_t[m, :, 0:RHS] = fold(dot(lhs, rhs, 0, 0))
    mid_split = [even_odd(mid_t, m) for m in range(MID_DEV)]
    for m in range(MID_DEV):
        packed[COEF_ROW:, 128 * (LEAF_DEV + m) : 128 * (LEAF_DEV + m) + 128] = pack(mid_split[m])
    lhs = jnp.concatenate([mid_rows[pl.ds(m, CHUNKS, stride=8), :] for m in range(MID_DEV)], axis=0)
    rhs = jnp.concatenate(mid_split, axis=0)
    leaf_t[0, :, 0:RHS] = fold(dot(lhs, rhs, 0, 0))
    tile = pack(even_odd(leaf_t, 0))
    for peer in range(top_out.shape[0]):
        top_out[peer] = tile


def up_call(dens, points, normals, col_basis, up_leaf, up_mid, peers):
    return pl.pallas_call(
        up_kernel,
        name="up_sweep",
        out_shape=(
            jax.ShapeDtypeStruct((peers, 8, 128), f32),
            jax.ShapeDtypeStruct((PACKED_ROWS, SPAN), f32),
        ),
        in_specs=[VMEM] * 6,
        out_specs=(VMEM, VMEM),
        scratch_shapes=[
            pltpu.VMEM((8 * CHUNKS, 128), f32),
            pltpu.VMEM((8 * CHUNKS, 128), f32),
            pltpu.VMEM((LEAF_DEV, RANK, 128), f32),
            pltpu.VMEM((MID_DEV, RANK, 128), f32),
        ],
        cost_estimate=pl.CostEstimate(flops=10_000_000, bytes_accessed=800_000, transcendentals=0),
    )(dens, points, normals, col_basis, up_leaf, up_mid)


def three_parts(values):
    first = values.astype(bf16).astype(f32)
    rest = values - first
    second = rest.astype(bf16).astype(f32)
    return first, second, (rest - second).astype(bf16).astype(f32)


def near_kernel(
    near_list,
    near_count,
    adm_leaf,
    adm_mid,
    own,
    low,
    high,
    couple_leaf,
    couple_mid,
    couple_top,
    down_mid,
    down_leaf,
    near_out,
    leaf_couple,
    mid_couple,
    top_mats,
    mid_mats,
    leaf_mats,
    feats,
    sources,
    targets,
    dens_parts,
    split_leaf,
    split_mid,
    rows,
    natural,
    work,
):
    halo = (low, own, high)
    first_leaf = near_list[0, 0]

    count = jnp.int32(0)
    for i in range(LEAF_DEV):
        limit = near_count[i]
        slots = [near_list[i, j] for j in range(NEAR)]
        used = [jnp.int32(j) < limit for j in range(NEAR)]
        for j in range(NEAR):
            uses = jnp.int32(0)
            fresh = used[j]
            for other in range(NEAR):
                same = jnp.logical_and(used[other], slots[other] == slots[j])
                uses = uses + same.astype(jnp.int32)
                if other < j:
                    fresh = jnp.logical_and(fresh, jnp.logical_not(same))
            work[0, count] = jnp.int32(i)
            work[1, count] = slots[j] - first_leaf + LEAF_DEV
            work[2, count] = uses
            count = count + fresh.astype(jnp.int32)
    work[0, count] = jnp.int32(0)
    work[1, count] = jnp.int32(0)
    work[2, count] = jnp.int32(0)

    for side in range(3):
        block = halo[side]
        place = block[RHS : RHS + 3, :] - 0.5
        normal = block[RHS + 3 : RHS + 6, :] * (1.0 / four_pi)
        p1, p2, p3 = three_parts(place)
        n1, n2, n3 = three_parts(normal)
        square = jnp.sum(place * place, axis=0, keepdims=True)
        inner = -jnp.sum(place * normal, axis=0, keepdims=True)
        ones = jnp.ones((3, SPAN), f32)
        zeros = jnp.zeros((8, SPAN), f32)
        s1, s2, s3 = three_parts(square)
        i1, i2, i3 = three_parts(inner)
        feats[0:8] = zeros
        feats[24:32] = zeros
        feats[32:40] = zeros
        feats[56:64] = zeros
        feats[0:1], feats[1:2], feats[2:3] = s1, s2, s3
        feats[3:6] = ones
        for slot, part in enumerate((p1, p1, p2, p2, p1, p3)):
            feats[6 + 3 * slot : 9 + 3 * slot] = part * -2.0
        feats[32:33], feats[33:34], feats[34:35] = i1, i2, i3
        for slot, part in enumerate((n1, n1, n2, n2, n1, n3)):
            feats[38 + 3 * slot : 41 + 3 * slot] = part
        for leaf in range(LEAF_DEV):
            cols = slice(LEAF * leaf, LEAF * leaf + LEAF)
            start = (LEAF_DEV * side + leaf) * LEAF
            sources[start : start + LEAF, :] = jnp.transpose(feats[:, cols]).astype(bf16)
            dens = block[0:RHS, cols]
            dens_high = dens.astype(bf16)
            dens_parts[LEAF_DEV * side + leaf, 0:RHS, :] = dens_high
            dens_parts[LEAF_DEV * side + leaf, RHS:, :] = (dens - dens_high.astype(f32)).astype(bf16)
        if side == 1:
            t1, t2, t3 = three_parts(square + smooth_sq)
            feats[0:3] = ones
            feats[3:4], feats[4:5], feats[5:6] = t1, t2, t3
            for slot, part in enumerate((p1, p2, p1, p2, p3, p1)):
                feats[6 + 3 * slot : 9 + 3 * slot] = part
            feats[24:32] = zeros
            target = feats[0:FEATURES, :].astype(bf16)
            blank = jnp.zeros((FEATURES, LEAF), bf16)
            for leaf in range(LEAF_DEV):
                piece = target[:, LEAF * leaf : LEAF * leaf + LEAF]
                targets[leaf, 0:FEATURES, 0:LEAF] = piece
                targets[leaf, 0:FEATURES, LEAF:] = blank
                targets[leaf, FEATURES:, 0:LEAF] = blank
                targets[leaf, FEATURES:, LEAF:] = piece

    for leaf in range(LEAF_DEV):
        near_out[leaf] = 0.5 * own[0:RHS, LEAF * leaf : LEAF * leaf + LEAF]

    def one_block(entry):
        leaf = work[0, entry]
        source = work[1, entry]
        uses = work[2, entry].astype(f32)
        start = pl.multiple_of(source * LEAF, LEAF)
        both = lax.dot_general(
            sources[pl.ds(start, LEAF), :],
            targets[leaf],
            (((1,), (0,)), ((), ())),
            preferred_element_type=f32,
        )
        inverse = lax.rsqrt(both[:, :LEAF])
        block = both[:, LEAF:] * (inverse * inverse * inverse)
        block_high = block.astype(bf16)
        block_low = (block - block_high.astype(f32)).astype(bf16)
        dens = dens_parts[source]
        first = lax.dot_general(dens, block_high, (((1,), (0,)), ((), ())), preferred_element_type=f32)
        second = lax.dot_general(dens[:RHS], block_low, (((1,), (0,)), ((), ())), preferred_element_type=f32)
        return leaf, uses * (first[:RHS] + first[RHS:] + second)

    def two_blocks(step, carry):
        leaf_a, term_a = one_block(2 * step)
        leaf_b, term_b = one_block(2 * step + 1)
        near_out[leaf_a] = near_out[leaf_a] + term_a
        near_out[leaf_b] = near_out[leaf_b] + term_b
        return carry

    lax.fori_loop(0, (count + 1) // 2, two_blocks, 0)

    for side in range(3):
        for c in range(LEAF_DEV):
            split_leaf[LEAF_DEV * side + c] = unpack(halo[side][COEF_ROW:, 128 * c : 128 * c + 128])
        for m in range(MID_DEV):
            lanes = slice(128 * (LEAF_DEV + m), 128 * (LEAF_DEV + m) + 128)
            split_mid[MID_DEV * side + m] = unpack(halo[side][COEF_ROW:, lanes])
    first_mid = first_leaf // 2
    for t in range(LEAF_DEV):
        for chunk in range(CHUNKS):
            rows[8 * chunk : 8 * chunk + ADM_LEAF, :] = couple_leaf[t, :, 128 * chunk : 128 * chunk + 128]
        lhs = jnp.concatenate([rows[pl.ds(a, CHUNKS, stride=8), :] for a in range(ADM_LEAF)], axis=0)
        rhs = jnp.concatenate(
            [split_leaf[adm_leaf[t, a] - first_leaf + LEAF_DEV] for a in range(ADM_LEAF)], axis=0
        )
        leaf_couple[t] = fold(dot(lhs, rhs, 0, 0))
    for t in range(MID_DEV):
        for chunk in range(CHUNKS):
            rows[8 * chunk : 8 * chunk + ADM_MID, :] = couple_mid[t, :, 128 * chunk : 128 * chunk + 128]
        lhs = jnp.concatenate([rows[pl.ds(a, CHUNKS, stride=8), :] for a in range(ADM_MID)], axis=0)
        rhs = jnp.concatenate(
            [split_mid[adm_mid[t, a] - first_mid + MID_DEV] for a in range(ADM_MID)], axis=0
        )
        mid_couple[t] = fold(dot(lhs, rhs, 0, 0))

    for chunk in range(CHUNKS):
        rows[16 * chunk : 16 * chunk + ADM_TOP, :] = couple_top[0, :, 128 * chunk : 128 * chunk + 128]
    for group in range(4):
        stack = jnp.concatenate(
            [rows[pl.ds(4 * group + a, CHUNKS, stride=16), :] for a in range(4)], axis=0
        )
        top_mats[:, 128 * group : 128 * group + 128] = jnp.transpose(stack)
    for source, result, number in ((down_mid, mid_mats, MID_DEV), (down_leaf, leaf_mats, LEAF_DEV)):
        for chunk in range(CHUNKS):
            rows[8 * chunk : 8 * chunk + number, :] = source[:, 128 * chunk : 128 * chunk + 128]
        for c in range(number):
            wide = rows[pl.ds(c, CHUNKS, stride=8), :]
            swapped = jnp.concatenate([wide[:, RANK:], wide[:, :RANK]], axis=1)
            natural[pl.ds(0, HALF, stride=2), :] = wide
            natural[pl.ds(1, HALF, stride=2), :] = swapped
            result[c] = jnp.transpose(natural[...])[:RANK]


def near_call(near_list, near_count, adm_leaf, adm_mid, own, low, high, couple_leaf, couple_mid, couple_top, down_mid, down_leaf):
    return pl.pallas_call(
        near_kernel,
        name="near_and_couplings",
        out_shape=(
            jax.ShapeDtypeStruct((LEAF_DEV, RHS, LEAF), f32),
            jax.ShapeDtypeStruct((LEAF_DEV, RANK, RHS), f32),
            jax.ShapeDtypeStruct((MID_DEV, RANK, RHS), f32),
            jax.ShapeDtypeStruct((128, ADM_TOP * HALF), f32),
            jax.ShapeDtypeStruct((MID_DEV, RANK, RANK), f32),
            jax.ShapeDtypeStruct((LEAF_DEV, RANK, RANK), f32),
        ),
        in_specs=[SMEM] * 4 + [VMEM] * 8,
        out_specs=(VMEM,) * 6,
        scratch_shapes=[
            pltpu.VMEM((2 * FEATURES, SPAN), f32),
            pltpu.VMEM((3 * SPAN, 2 * FEATURES), bf16),
            pltpu.VMEM((LEAF_DEV, 2 * FEATURES, 2 * LEAF), bf16),
            pltpu.VMEM((3 * LEAF_DEV, 2 * RHS, LEAF), bf16),
            pltpu.VMEM((3 * LEAF_DEV, HALF, HALF), f32),
            pltpu.VMEM((3 * MID_DEV, HALF, HALF), f32),
            pltpu.VMEM((16 * CHUNKS, 128), f32),
            pltpu.VMEM((RANK, 128), f32),
            pltpu.SMEM((3, LEAF_DEV * NEAR + 8), jnp.int32),
        ],
        compiler_params=pltpu.CompilerParams(vmem_limit_bytes=32 * 1024 * 1024),
        cost_estimate=pl.CostEstimate(flops=4_000_000_000, bytes_accessed=2_000_000, transcendentals=2_000_000),
    )(near_list, near_count, adm_leaf, adm_mid, own, low, high, couple_leaf, couple_mid, couple_top, down_mid, down_leaf)


def down_kernel(
    adm_top,
    near_list,
    own_tops,
    other_tops,
    near_part,
    leaf_couple,
    mid_couple,
    top_mats,
    mid_mats,
    leaf_mats,
    row_basis,
    out,
    tiles,
    sems,
):
    core = (near_list[0, 0] // LEAF_DEV) % 2
    for a in range(ADM_TOP):
        top = adm_top[0, a]
        mine = top % 2 == core
        row = top // 2

        @pl.when(mine)
        def _():
            pltpu.make_async_copy(own_tops.at[row], tiles.at[a], sems.at[a]).start()

        @pl.when(jnp.logical_not(mine))
        def _():
            pltpu.make_async_copy(other_tops.at[row], tiles.at[a], sems.at[a]).start()

    for a in range(ADM_TOP):
        pltpu.make_async_copy(own_tops.at[0], tiles.at[a], sems.at[a]).wait()
    chosen = jnp.concatenate([unpack(tiles[a]) for a in range(ADM_TOP)], axis=0)
    top_field = fold(dot(top_mats[...], chosen))
    for m in range(MID_DEV):
        mid_field = mid_couple[m] + dot(mid_mats[m], top_field)
        for c in (2 * m, 2 * m + 1):
            leaf_field = leaf_couple[c] + dot(leaf_mats[c], mid_field)
            cols = slice(LEAF * c, LEAF * c + LEAF)
            out[:, cols] = near_part[c] + dot(leaf_field, row_basis[:, cols], 0, 0)


def down_call(adm_top, near_list, own_tops, other_tops, *rest):
    return pl.pallas_call(
        down_kernel,
        name="down_sweep",
        out_shape=jax.ShapeDtypeStruct((RHS, SPAN), f32),
        in_specs=[SMEM] * 2 + [ANY] * 2 + [VMEM] * 7,
        out_specs=VMEM,
        scratch_shapes=[pltpu.VMEM((ADM_TOP, 8, 128), f32), pltpu.SemaphoreType.DMA((ADM_TOP,))],
        cost_estimate=pl.CostEstimate(flops=10_000_000, bytes_accessed=800_000, transcendentals=0),
    )(adm_top, near_list, own_tops, other_tops, *rest)


def solution(mesh):
    devices = mesh.devices.size
    cores = 2
    ring = 16
    planes = devices // (cores * ring)
    along_z = [
        [(plane * ring + z) * cores + core for z in range(ring)] for plane in range(planes) for core in range(cores)
    ]
    across = [
        [(plane * ring + z) * cores + core for plane in range(planes)] for z in range(ring) for core in range(cores)
    ]

    def on_device(
        densities,
        points,
        area_normals,
        col_basis,
        row_basis,
        up_leaf,
        up_mid,
        down_leaf,
        down_mid,
        couple_leaf,
        couple_mid,
        couple_top,
        near_list,
        near_count,
        adm_leaf,
        adm_mid,
        adm_top,
    ):
        own_top, packed = up_call(densities, points, area_normals, col_basis, up_leaf, up_mid, ring)
        ring_tops = lax.all_to_all(own_top, "leaf", 0, 0, axis_index_groups=along_z, tiled=True)
        low = lax.ppermute(packed, "leaf", [(i, (i + 1) % devices) for i in range(devices)])
        high = lax.ppermute(packed, "leaf", [((i + 1) % devices, i) for i in range(devices)])
        spread = jnp.broadcast_to(ring_tops.reshape(1, ring * 8, 128), (planes, ring * 8, 128))
        core_tops = lax.all_to_all(spread, "leaf", 0, 0, axis_index_groups=across, tiled=True)
        other_tops = lax.ppermute(core_tops, "leaf", [(i, i ^ 1) for i in range(devices)])
        near_part, leaf_couple, mid_couple, top_mats, mid_mats, leaf_mats = near_call(
            near_list, near_count, adm_leaf, adm_mid, packed, low, high, couple_leaf, couple_mid, couple_top, down_mid, down_leaf
        )
        return down_call(
            adm_top,
            near_list,
            core_tops.reshape(planes * ring, 8, 128),
            other_tops.reshape(planes * ring, 8, 128),
            near_part,
            leaf_couple,
            mid_couple,
            top_mats,
            mid_mats,
            leaf_mats,
            row_basis,
        )

    split_last = P(None, "leaf")
    split_first = P("leaf", None)
    split_three = P("leaf", None, None)
    return jax.shard_map(
        on_device,
        mesh=mesh,
        in_specs=(split_last,) * 5
        + (split_first,) * 4
        + (split_three,) * 3
        + (split_first, P("leaf"), split_first, split_first, split_first),
        out_specs=split_last,
        check_vma=False,
    )
```

```python
import math

import jax
import jax.numpy as jnp
from jax import lax
from jax.experimental import pallas as pl
from jax.experimental.pallas import tpu as pltpu
from jax.sharding import PartitionSpec as P

RHS = 16
LEAF = 256
RANK = 64
HALF = RANK // 2
LEAF_DEV = 4
MID_DEV = 2
NEAR = 8
ADM_LEAF = 6
ADM_MID = 6
ADM_TOP = 16
SPAN = LEAF_DEV * LEAF
CHUNKS = RANK * RANK // 128
FEATURES = 32
PACKED_ROWS = 32
COEF_ROW = 24
VMEM_LIMIT = 16 * 1024 * 1024

smooth_sq = 0.01
four_pi = 4.0 * math.pi
highest = lax.Precision.HIGHEST
f32 = jnp.float32
bf16 = jnp.bfloat16

SMEM = pl.BlockSpec(memory_space=pltpu.SMEM)
VMEM = pl.BlockSpec(memory_space=pltpu.VMEM)


def dot(lhs, rhs, lhs_dim=1, rhs_dim=0):
    return lax.dot_general(
        lhs,
        rhs,
        (((lhs_dim,), (rhs_dim,)), ((), ())),
        precision=highest,
        preferred_element_type=f32,
    )


def even_odd(ref, index):
    even = ref[index, pl.ds(0, HALF, stride=2), :]
    odd = ref[index, pl.ds(1, HALF, stride=2), :]
    return jnp.concatenate([even[:, :RHS], odd[:, :RHS]], axis=1)


def pack(split):
    return jnp.concatenate([split[8 * g : 8 * g + 8] for g in range(4)], axis=1)


def unpack(tile):
    return jnp.concatenate([tile[:, 32 * g : 32 * g + 32] for g in range(4)], axis=0)


def fold(product):
    return product[:RANK, :RHS] + product[RANK:, RHS:]


def up_kernel(dens, points, normals, col_basis, up_leaf, up_mid, top_out, packed, leaf_rows, mid_rows, leaf_t, mid_t):
    packed[0:RHS, :] = dens[...]
    packed[RHS : RHS + 3, :] = points[...]
    packed[RHS + 3 : RHS + 6, :] = normals[...]
    packed[RHS + 6 : COEF_ROW, :] = jnp.zeros((COEF_ROW - RHS - 6, SPAN), f32)
    packed[COEF_ROW:, 6 * 128 :] = jnp.zeros((8, SPAN - 6 * 128), f32)
    for chunk in range(CHUNKS):
        lanes = slice(128 * chunk, 128 * chunk + 128)
        leaf_rows[8 * chunk : 8 * chunk + LEAF_DEV, :] = up_leaf[:, lanes]
        mid_rows[8 * chunk : 8 * chunk + MID_DEV, :] = up_mid[:, lanes]
    for c in range(LEAF_DEV):
        cols = slice(LEAF * c, LEAF * c + LEAF)
        leaf_t[c, :, 0:RHS] = dot(col_basis[:, cols], dens[:, cols], 1, 1)
    leaf_split = [even_odd(leaf_t, c) for c in range(LEAF_DEV)]
    for c in range(LEAF_DEV):
        packed[COEF_ROW:, 128 * c : 128 * c + 128] = pack(leaf_split[c])
    for m in range(MID_DEV):
        pair = (2 * m, 2 * m + 1)
        lhs = jnp.concatenate([leaf_rows[pl.ds(c, CHUNKS, stride=8), :] for c in pair], axis=0)
        rhs = jnp.concatenate([leaf_split[c] for c in pair], axis=0)
        mid_t[m, :, 0:RHS] = fold(dot(lhs, rhs, 0, 0))
    mid_split = [even_odd(mid_t, m) for m in range(MID_DEV)]
    for m in range(MID_DEV):
        packed[COEF_ROW:, 128 * (LEAF_DEV + m) : 128 * (LEAF_DEV + m) + 128] = pack(mid_split[m])
    lhs = jnp.concatenate([mid_rows[pl.ds(m, CHUNKS, stride=8), :] for m in range(MID_DEV)], axis=0)
    rhs = jnp.concatenate(mid_split, axis=0)
    leaf_t[0, :, 0:RHS] = fold(dot(lhs, rhs, 0, 0))
    tile = pack(even_odd(leaf_t, 0))
    for peer in range(top_out.shape[0]):
        top_out[peer] = tile


def up_call(dens, points, normals, col_basis, up_leaf, up_mid, peers):
    return pl.pallas_call(
        up_kernel,
        name="up_sweep",
        out_shape=(
            jax.ShapeDtypeStruct((peers, 8, 128), f32),
            jax.ShapeDtypeStruct((PACKED_ROWS, SPAN), f32),
        ),
        in_specs=[VMEM] * 6,
        out_specs=(VMEM, VMEM),
        scratch_shapes=[
            pltpu.VMEM((8 * CHUNKS, 128), f32),
            pltpu.VMEM((8 * CHUNKS, 128), f32),
            pltpu.VMEM((LEAF_DEV, RANK, 128), f32),
            pltpu.VMEM((MID_DEV, RANK, 128), f32),
        ],
        cost_estimate=pl.CostEstimate(flops=10_000_000, bytes_accessed=800_000, transcendentals=0),
    )(dens, points, normals, col_basis, up_leaf, up_mid)


def two_parts(values):
    first = values.astype(bf16)
    return first, (values - first.astype(f32)).astype(bf16)


def bf16_dot(lhs, rhs):
    return lax.dot_general(lhs, rhs, (((1,), (0,)), ((), ())), preferred_element_type=f32)


def three_parts(values):
    first = values.astype(bf16).astype(f32)
    rest = values - first
    second = rest.astype(bf16).astype(f32)
    return first, second, (rest - second).astype(bf16).astype(f32)


def near_kernel(
    near_list,
    near_count,
    adm_leaf,
    adm_mid,
    own,
    same_chip,
    next_chip,
    couple_leaf,
    couple_mid,
    leaf_mats,
    row_basis,
    adm_top,
    base,
    picks,
    near_out,
    leaf_couple,
    mid_couple,
    feats,
    sources,
    targets,
    dens_parts,
    split_leaf,
    split_mid,
    rows,
    work,
):
    halo = (same_chip, own, next_chip)
    first_leaf = near_list[0, 0]
    first_mid = first_leaf // 2
    core = (first_leaf // LEAF_DEV) % 2

    def held(place, number):
        side = place // number
        return jnp.where(core == 0, place + (2 - 2 * side) * number, place)

    for a in range(ADM_TOP):
        picks[0, a] = adm_top[0, a] // 2
        picks[1, a] = (adm_top[0, a] % 2 == core).astype(jnp.int32)

    count = jnp.int32(0)
    for i in range(LEAF_DEV):
        limit = near_count[i]
        slots = [near_list[i, j] for j in range(NEAR)]
        used = [jnp.int32(j) < limit for j in range(NEAR)]
        for j in range(NEAR):
            uses = jnp.int32(0)
            fresh = used[j]
            for other in range(NEAR):
                same = jnp.logical_and(used[other], slots[other] == slots[j])
                uses = uses + same.astype(jnp.int32)
                if other < j:
                    fresh = jnp.logical_and(fresh, jnp.logical_not(same))
            work[0, count] = jnp.int32(i)
            work[1, count] = held(slots[j] - first_leaf + LEAF_DEV, LEAF_DEV)
            work[2, count] = uses
            count = count + fresh.astype(jnp.int32)
    work[0, count] = jnp.int32(0)
    work[1, count] = jnp.int32(0)
    work[2, count] = jnp.int32(0)

    for side in range(3):
        block = halo[side]
        place = block[RHS : RHS + 3, :] - 0.5
        normal = block[RHS + 3 : RHS + 6, :] * (1.0 / four_pi)
        p1, p2, p3 = three_parts(place)
        n1, n2, n3 = three_parts(normal)
        square = jnp.sum(place * place, axis=0, keepdims=True)
        inner = -jnp.sum(place * normal, axis=0, keepdims=True)
        ones = jnp.ones((3, SPAN), f32)
        zeros = jnp.zeros((8, SPAN), f32)
        s1, s2, s3 = three_parts(square)
        i1, i2, i3 = three_parts(inner)
        feats[0:8] = zeros
        feats[24:32] = zeros
        feats[32:40] = zeros
        feats[56:64] = zeros
        feats[0:1], feats[1:2], feats[2:3] = s1, s2, s3
        feats[3:6] = ones
        for slot, part in enumerate((p1, p1, p2, p2, p1, p3)):
            feats[6 + 3 * slot : 9 + 3 * slot] = part * -2.0
        feats[32:33], feats[33:34], feats[34:35] = i1, i2, i3
        for slot, part in enumerate((n1, n1, n2, n2, n1, n3)):
            feats[38 + 3 * slot : 41 + 3 * slot] = part
        for leaf in range(LEAF_DEV):
            cols = slice(LEAF * leaf, LEAF * leaf + LEAF)
            start = (LEAF_DEV * side + leaf) * LEAF
            sources[start : start + LEAF, :] = jnp.transpose(feats[:, cols]).astype(bf16)
            dens = block[0:RHS, cols]
            dens_high = dens.astype(bf16)
            dens_parts[LEAF_DEV * side + leaf, 0:RHS, :] = dens_high
            dens_parts[LEAF_DEV * side + leaf, RHS:, :] = (dens - dens_high.astype(f32)).astype(bf16)
        if side == 1:
            t1, t2, t3 = three_parts(square + smooth_sq)
            feats[0:3] = ones
            feats[3:4], feats[4:5], feats[5:6] = t1, t2, t3
            for slot, part in enumerate((p1, p2, p1, p2, p3, p1)):
                feats[6 + 3 * slot : 9 + 3 * slot] = part
            feats[24:32] = zeros
            target = feats[0:FEATURES, :].astype(bf16)
            blank = jnp.zeros((FEATURES, LEAF), bf16)
            for leaf in range(LEAF_DEV):
                piece = target[:, LEAF * leaf : LEAF * leaf + LEAF]
                targets[leaf, 0:FEATURES, 0:LEAF] = piece
                targets[leaf, 0:FEATURES, LEAF:] = blank
                targets[leaf, FEATURES:, 0:LEAF] = blank
                targets[leaf, FEATURES:, LEAF:] = piece

    for leaf in range(LEAF_DEV):
        near_out[leaf] = 0.5 * own[0:RHS, LEAF * leaf : LEAF * leaf + LEAF]

    def one_block(entry):
        leaf = work[0, entry]
        source = work[1, entry]
        uses = work[2, entry].astype(f32)
        start = pl.multiple_of(source * LEAF, LEAF)
        both = lax.dot_general(
            sources[pl.ds(start, LEAF), :],
            targets[leaf],
            (((1,), (0,)), ((), ())),
            preferred_element_type=f32,
        )
        inverse = lax.rsqrt(both[:, :LEAF])
        block = both[:, LEAF:] * (inverse * inverse * inverse)
        block_high = block.astype(bf16)
        block_low = (block - block_high.astype(f32)).astype(bf16)
        dens = dens_parts[source]
        first = lax.dot_general(dens, block_high, (((1,), (0,)), ((), ())), preferred_element_type=f32)
        second = lax.dot_general(dens[:RHS], block_low, (((1,), (0,)), ((), ())), preferred_element_type=f32)
        return leaf, uses * (first[:RHS] + first[RHS:] + second)

    def two_blocks(step, carry):
        leaf_a, term_a = one_block(2 * step)
        leaf_b, term_b = one_block(2 * step + 1)
        near_out[leaf_a] = near_out[leaf_a] + term_a
        near_out[leaf_b] = near_out[leaf_b] + term_b
        return carry

    lax.fori_loop(0, (count + 1) // 2, two_blocks, 0)

    for side in range(3):
        for c in range(LEAF_DEV):
            split_leaf[LEAF_DEV * side + c] = unpack(halo[side][COEF_ROW:, 128 * c : 128 * c + 128])
        for m in range(MID_DEV):
            lanes = slice(128 * (LEAF_DEV + m), 128 * (LEAF_DEV + m) + 128)
            split_mid[MID_DEV * side + m] = unpack(halo[side][COEF_ROW:, lanes])
    for t in range(LEAF_DEV):
        for chunk in range(CHUNKS):
            rows[8 * chunk : 8 * chunk + ADM_LEAF, :] = couple_leaf[t, :, 128 * chunk : 128 * chunk + 128]
        lhs = jnp.concatenate([rows[pl.ds(a, CHUNKS, stride=8), :] for a in range(ADM_LEAF)], axis=0)
        rhs = jnp.concatenate(
            [split_leaf[held(adm_leaf[t, a] - first_leaf + LEAF_DEV, LEAF_DEV)] for a in range(ADM_LEAF)], axis=0
        )
        leaf_couple[t] = fold(dot(lhs, rhs, 0, 0))
    for t in range(MID_DEV):
        for chunk in range(CHUNKS):
            rows[8 * chunk : 8 * chunk + ADM_MID, :] = couple_mid[t, :, 128 * chunk : 128 * chunk + 128]
        lhs = jnp.concatenate([rows[pl.ds(a, CHUNKS, stride=8), :] for a in range(ADM_MID)], axis=0)
        rhs = jnp.concatenate(
            [split_mid[held(adm_mid[t, a] - first_mid + MID_DEV, MID_DEV)] for a in range(ADM_MID)], axis=0
        )
        mid_couple[t] = fold(dot(lhs, rhs, 0, 0))
    for c in range(LEAF_DEV):
        cols = slice(LEAF * c, LEAF * c + LEAF)
        field = leaf_couple[c] + dot(leaf_mats[c], mid_couple[c // 2])
        base[:, cols] = near_out[c] + dot(field, row_basis[:, cols], 0, 0)


def matrix_kernel(couple_top, down_mid, down_leaf, row_basis, top_mats, leaf_mats, top_to_points, mid_mats, rows, natural):
    for chunk in range(CHUNKS):
        rows[16 * chunk : 16 * chunk + ADM_TOP, :] = couple_top[0, :, 128 * chunk : 128 * chunk + 128]
    for group in range(4):
        stack = jnp.concatenate(
            [rows[pl.ds(4 * group + a, CHUNKS, stride=16), :] for a in range(4)], axis=0
        )
        high, low = two_parts(jnp.transpose(stack))
        top_mats[0:128, 128 * group : 128 * group + 128] = high
        top_mats[128:, 128 * group : 128 * group + 128] = low
    for source, result, number in ((down_mid, mid_mats, MID_DEV), (down_leaf, leaf_mats, LEAF_DEV)):
        for chunk in range(CHUNKS):
            rows[8 * chunk : 8 * chunk + number, :] = source[:, 128 * chunk : 128 * chunk + 128]
        for c in range(number):
            wide = rows[pl.ds(c, CHUNKS, stride=8), :]
            swapped = jnp.concatenate([wide[:, RANK:], wide[:, :RANK]], axis=1)
            natural[pl.ds(0, HALF, stride=2), :] = wide
            natural[pl.ds(1, HALF, stride=2), :] = swapped
            result[c] = jnp.transpose(natural[...])[:RANK]
    for c in range(LEAF_DEV):
        cols = slice(LEAF * c, LEAF * c + LEAF)
        high, low = two_parts(dot(dot(leaf_mats[c], mid_mats[c // 2]), row_basis[:, cols], 0, 0))
        top_to_points[0:RANK, cols] = high
        top_to_points[RANK : 2 * RANK, cols] = high
        top_to_points[2 * RANK :, cols] = low


def matrix_call(*operands):
    return pl.pallas_call(
        matrix_kernel,
        name="transposed_matrices",
        out_shape=(
            jax.ShapeDtypeStruct((256, ADM_TOP * HALF), bf16),
            jax.ShapeDtypeStruct((LEAF_DEV, RANK, RANK), f32),
            jax.ShapeDtypeStruct((3 * RANK, SPAN), bf16),
        ),
        in_specs=[VMEM] * 4,
        out_specs=(VMEM,) * 3,
        scratch_shapes=[
            pltpu.VMEM((MID_DEV, RANK, RANK), f32),
            pltpu.VMEM((16 * CHUNKS, 128), f32),
            pltpu.VMEM((RANK, 128), f32),
        ],
        compiler_params=pltpu.CompilerParams(vmem_limit_bytes=VMEM_LIMIT),
        cost_estimate=pl.CostEstimate(flops=2_000_000_000, bytes_accessed=2_000_000, transcendentals=0),
    )(*operands)


def near_call(near_list, near_count, adm_leaf, adm_mid, *rest):
    return pl.pallas_call(
        near_kernel,
        name="near_and_couplings",
        out_shape=(
            jax.ShapeDtypeStruct((RHS, SPAN), f32),
            jax.ShapeDtypeStruct((2, ADM_TOP), jnp.int32),
        ),
        in_specs=[SMEM] * 4 + [VMEM] * 7 + [SMEM],
        out_specs=(VMEM, SMEM),
        scratch_shapes=[
            pltpu.VMEM((LEAF_DEV, RHS, LEAF), f32),
            pltpu.VMEM((LEAF_DEV, RANK, RHS), f32),
            pltpu.VMEM((MID_DEV, RANK, RHS), f32),
            pltpu.VMEM((2 * FEATURES, SPAN), f32),
            pltpu.VMEM((3 * SPAN, 2 * FEATURES), bf16),
            pltpu.VMEM((LEAF_DEV, 2 * FEATURES, 2 * LEAF), bf16),
            pltpu.VMEM((3 * LEAF_DEV, 2 * RHS, LEAF), bf16),
            pltpu.VMEM((3 * LEAF_DEV, HALF, HALF), f32),
            pltpu.VMEM((3 * MID_DEV, HALF, HALF), f32),
            pltpu.VMEM((8 * CHUNKS, 128), f32),
            pltpu.SMEM((3, LEAF_DEV * NEAR + 8), jnp.int32),
        ],
        compiler_params=pltpu.CompilerParams(vmem_limit_bytes=VMEM_LIMIT),
        cost_estimate=pl.CostEstimate(flops=4_000_000_000, bytes_accessed=2_000_000, transcendentals=2_000_000),
    )(near_list, near_count, adm_leaf, adm_mid, *rest)


def down_kernel(picks, own_tops, other_tops, base, top_mats, top_to_points, out):
    tiles = []
    for a in range(ADM_TOP):
        row = picks[0, a]
        tiles.append(jnp.where(picks[1, a] == 1, own_tops[row], other_tops[row]))
    chosen = jnp.concatenate([unpack(tile) for tile in tiles], axis=0)
    high, low = two_parts(chosen)
    product = bf16_dot(top_mats[...], jnp.concatenate([high, low], axis=1))
    width = 2 * RHS
    top_field = fold(product[:128, :width] + product[:128, width:] + product[128:, :width])
    high, low = two_parts(jnp.transpose(top_field))
    out[...] = base[...] + bf16_dot(jnp.concatenate([high, low, high], axis=1), top_to_points[...])


def down_call(*operands):
    return pl.pallas_call(
        down_kernel,
        name="down_sweep",
        out_shape=jax.ShapeDtypeStruct((RHS, SPAN), f32),
        in_specs=[SMEM] + [VMEM] * 5,
        out_specs=VMEM,
        compiler_params=pltpu.CompilerParams(vmem_limit_bytes=VMEM_LIMIT),
        cost_estimate=pl.CostEstimate(flops=10_000_000, bytes_accessed=800_000, transcendentals=0),
    )(*operands)


def solution(mesh):
    devices = mesh.devices.size
    cores = 2
    ring = 16
    planes = devices // (cores * ring)
    along_z = [
        [(plane * ring + z) * cores + core for z in range(ring)] for plane in range(planes) for core in range(cores)
    ]
    across = [
        [(plane * ring + z) * cores + core for plane in range(planes)] for z in range(ring) for core in range(cores)
    ]

    def on_device(
        densities,
        points,
        area_normals,
        col_basis,
        row_basis,
        up_leaf,
        up_mid,
        down_leaf,
        down_mid,
        couple_leaf,
        couple_mid,
        couple_top,
        near_list,
        near_count,
        adm_leaf,
        adm_mid,
        adm_top,
    ):
        own_top, packed = up_call(densities, points, area_normals, col_basis, up_leaf, up_mid, ring)
        own_top, couple_top, down_mid, down_leaf = lax.optimization_barrier((own_top, couple_top, down_mid, down_leaf))
        ring_tops = lax.all_to_all(own_top, "leaf", 0, 0, axis_index_groups=along_z, tiled=True)
        same_chip = lax.ppermute(packed, "leaf", [(i, i ^ 1) for i in range(devices)])
        next_chip = lax.ppermute(packed, "leaf", [(i, ((i + 1) ^ 1) - 1) for i in range(1, devices - 1)])
        top_mats, leaf_mats, top_to_points = matrix_call(couple_top, down_mid, down_leaf, row_basis)
        ring_tops, same_chip, next_chip, top_mats, leaf_mats, top_to_points = lax.optimization_barrier(
            (ring_tops, same_chip, next_chip, top_mats, leaf_mats, top_to_points)
        )
        spread = jnp.broadcast_to(ring_tops.reshape(1, ring * 8, 128), (planes, ring * 8, 128))
        core_tops = lax.all_to_all(spread, "leaf", 0, 0, axis_index_groups=across, tiled=True)
        base, picks = near_call(
            near_list,
            near_count,
            adm_leaf,
            adm_mid,
            packed,
            same_chip,
            next_chip,
            couple_leaf,
            couple_mid,
            leaf_mats,
            row_basis,
            adm_top,
        )
        core_tops, base, picks = lax.optimization_barrier((core_tops, base, picks))
        other_tops = lax.ppermute(core_tops, "leaf", [(i, i ^ 1) for i in range(devices)])
        return down_call(
            picks,
            core_tops.reshape(planes * ring, 8, 128),
            other_tops.reshape(planes * ring, 8, 128),
            base,
            top_mats,
            top_to_points,
        )

    split_last = P(None, "leaf")
    split_first = P("leaf", None)
    split_three = P("leaf", None, None)
    return jax.shard_map(
        on_device,
        mesh=mesh,
        in_specs=(split_last,) * 5
        + (split_first,) * 4
        + (split_three,) * 3
        + (split_first, P("leaf"), split_first, split_first, split_first),
        out_specs=split_last,
        check_vma=False,
    )
```

```python
import math

import jax
import jax.numpy as jnp
from jax import lax
from jax.experimental import pallas as pl
from jax.experimental.pallas import tpu as pltpu
from jax.sharding import PartitionSpec as P

RHS = 16
LEAF = 256
RANK = 64
HALF = RANK // 2
LEAF_DEV = 4
MID_DEV = 2
NEAR = 8
ADM_LEAF = 6
ADM_MID = 6
ADM_TOP = 16
SPAN = LEAF_DEV * LEAF
CHUNKS = RANK * RANK // 128
FEATURES = 32
PACKED_ROWS = 32
WANTED_ROW = 22
COEF_ROW = 24
GROUP = 8
VMEM_LIMIT = 16 * 1024 * 1024

smooth_sq = 0.01
four_pi = 4.0 * math.pi
highest = lax.Precision.HIGHEST
f32 = jnp.float32
bf16 = jnp.bfloat16

SMEM = pl.BlockSpec(memory_space=pltpu.SMEM)
VMEM = pl.BlockSpec(memory_space=pltpu.VMEM)


def dot(lhs, rhs, lhs_dim=1, rhs_dim=0):
    return lax.dot_general(
        lhs,
        rhs,
        (((lhs_dim,), (rhs_dim,)), ((), ())),
        precision=highest,
        preferred_element_type=f32,
    )


def even_odd(ref, index):
    even = ref[index, pl.ds(0, HALF, stride=2), :]
    odd = ref[index, pl.ds(1, HALF, stride=2), :]
    return jnp.concatenate([even[:, :RHS], odd[:, :RHS]], axis=1)


def pack(split):
    return jnp.concatenate([split[8 * g : 8 * g + 8] for g in range(4)], axis=1)


def unpack(tile):
    return jnp.concatenate([tile[:, 32 * g : 32 * g + 32] for g in range(4)], axis=0)


def fold(product):
    return product[:RANK, :RHS] + product[RANK:, RHS:]


def dot_parts(lhs, rhs, lhs_dim=1, rhs_dim=0):
    lhs_high, lhs_low = two_parts(lhs)
    rhs_high, rhs_low = two_parts(rhs)
    return lax.dot_general(
        jnp.concatenate([lhs_high, lhs_high, lhs_low], axis=lhs_dim),
        jnp.concatenate([rhs_high, rhs_low, rhs_high], axis=rhs_dim),
        (((lhs_dim,), (rhs_dim,)), ((), ())),
        preferred_element_type=f32,
    )


def up_kernel(dens, col_basis, up_leaf, up_mid, top_out, coefs, leaf_rows, mid_rows, leaf_t, mid_t):
    for chunk in range(CHUNKS):
        lanes = slice(128 * chunk, 128 * chunk + 128)
        leaf_rows[8 * chunk : 8 * chunk + LEAF_DEV, :] = up_leaf[:, lanes]
        mid_rows[8 * chunk : 8 * chunk + MID_DEV, :] = up_mid[:, lanes]
    for c in range(LEAF_DEV):
        cols = slice(LEAF * c, LEAF * c + LEAF)
        leaf_t[c, :, 0:RHS] = dot_parts(col_basis[:, cols], dens[:, cols], 1, 1)
    leaf_split = [even_odd(leaf_t, c) for c in range(LEAF_DEV)]
    for c in range(LEAF_DEV):
        coefs[:, 128 * c : 128 * c + 128] = pack(leaf_split[c])
    for m in range(MID_DEV):
        pair = (2 * m, 2 * m + 1)
        lhs = jnp.concatenate([leaf_rows[pl.ds(c, CHUNKS, stride=8), :] for c in pair], axis=0)
        rhs = jnp.concatenate([leaf_split[c] for c in pair], axis=0)
        mid_t[m, :, 0:RHS] = fold(dot_parts(lhs, rhs, 0, 0))
    mid_split = [even_odd(mid_t, m) for m in range(MID_DEV)]
    for m in range(MID_DEV):
        coefs[:, 128 * (LEAF_DEV + m) : 128 * (LEAF_DEV + m) + 128] = pack(mid_split[m])
    lhs = jnp.concatenate([mid_rows[pl.ds(m, CHUNKS, stride=8), :] for m in range(MID_DEV)], axis=0)
    rhs = jnp.concatenate(mid_split, axis=0)
    leaf_t[0, :, 0:RHS] = fold(dot_parts(lhs, rhs, 0, 0))
    tile = pack(even_odd(leaf_t, 0))
    for peer in range(top_out.shape[0]):
        top_out[peer] = tile


def pack_kernel(dens, points, normals, coefs, adm_top, packed):
    packed[0:RHS, :] = dens[...]
    packed[RHS : RHS + 3, :] = points[...]
    packed[RHS + 3 : RHS + 6, :] = normals[...]
    packed[WANTED_ROW:COEF_ROW, :] = jnp.zeros((COEF_ROW - WANTED_ROW, SPAN), f32)
    packed[WANTED_ROW : WANTED_ROW + 1, 0:ADM_TOP] = adm_top[...].astype(f32)
    packed[COEF_ROW:, 0 : 6 * 128] = coefs[...]
    packed[COEF_ROW:, 6 * 128 :] = jnp.zeros((8, SPAN - 6 * 128), f32)


def pack_call(*operands):
    return pl.pallas_call(
        pack_kernel,
        name="packed_for_neighbours",
        out_shape=jax.ShapeDtypeStruct((PACKED_ROWS, SPAN), f32),
        in_specs=[VMEM] * 5,
        out_specs=VMEM,
        compiler_params=pltpu.CompilerParams(vmem_limit_bytes=VMEM_LIMIT),
        cost_estimate=pl.CostEstimate(flops=100_000_000, bytes_accessed=400_000, transcendentals=0),
    )(*operands)


def up_call(dens, col_basis, up_leaf, up_mid, peers):
    return pl.pallas_call(
        up_kernel,
        name="up_sweep",
        out_shape=(
            jax.ShapeDtypeStruct((peers, 8, 128), f32),
            jax.ShapeDtypeStruct((8, 6 * 128), f32),
        ),
        in_specs=[VMEM] * 4,
        out_specs=(VMEM, VMEM),
        scratch_shapes=[
            pltpu.VMEM((8 * CHUNKS, 128), f32),
            pltpu.VMEM((8 * CHUNKS, 128), f32),
            pltpu.VMEM((LEAF_DEV, RANK, 128), f32),
            pltpu.VMEM((MID_DEV, RANK, 128), f32),
        ],
        cost_estimate=pl.CostEstimate(flops=10_000_000, bytes_accessed=800_000, transcendentals=0),
    )(dens, col_basis, up_leaf, up_mid)


def two_parts(values):
    first = values.astype(bf16)
    return first, (values - first.astype(f32)).astype(bf16)


def bf16_dot(lhs, rhs):
    return lax.dot_general(lhs, rhs, (((1,), (0,)), ((), ())), preferred_element_type=f32)


def three_parts(values):
    first = values.astype(bf16).astype(f32)
    rest = values - first
    second = rest.astype(bf16).astype(f32)
    return first, second, (rest - second).astype(bf16).astype(f32)


def near_kernel(
    near_list,
    near_count,
    adm_leaf,
    adm_mid,
    own,
    same_chip,
    next_chip,
    couple_leaf,
    couple_mid,
    leaf_mats,
    row_basis,
    adm_top,
    wanted,
    base,
    plan,
    near_out,
    near_t,
    leaf_couple,
    mid_couple,
    feats,
    sources,
    targets,
    dens_parts,
    split_leaf,
    split_mid,
    rows,
    work,
):
    halo = (same_chip, own, next_chip)
    first_leaf = near_list[0, 0]
    first_mid = first_leaf // 2
    core = (first_leaf // LEAF_DEV) % 2

    def held(place, number):
        side = place // number
        return jnp.where(core == 0, place + (2 - 2 * side) * number, place)

    for row, tops in ((0, adm_top), (2, wanted)):
        for a in range(ADM_TOP):
            plan[row, a] = tops[0, a] // 2
            plan[row + 1, a] = (tops[0, a] % 2 == core).astype(jnp.int32)

    count = jnp.int32(0)
    for i in range(LEAF_DEV):
        limit = near_count[i]
        slots = [near_list[i, j] for j in range(NEAR)]
        used = [jnp.int32(j) < limit for j in range(NEAR)]
        for j in range(NEAR):
            uses = jnp.int32(0)
            fresh = used[j]
            for other in range(NEAR):
                same = jnp.logical_and(used[other], slots[other] == slots[j])
                uses = uses + same.astype(jnp.int32)
                if other < j:
                    fresh = jnp.logical_and(fresh, jnp.logical_not(same))
            work[0, count] = jnp.int32(i)
            work[1, count] = held(slots[j] - first_leaf + LEAF_DEV, LEAF_DEV)
            work[2, count] = uses
            count = count + fresh.astype(jnp.int32)
    for extra in range(GROUP):
        work[0, count + extra] = jnp.int32(0)
        work[1, count + extra] = jnp.int32(0)
        work[2, count + extra] = jnp.int32(0)

    for side in range(3):
        block = halo[side]
        place = block[RHS : RHS + 3, :] - 0.5
        normal = block[RHS + 3 : RHS + 6, :] * (1.0 / four_pi)
        p1, p2, p3 = three_parts(place)
        n1, n2, n3 = three_parts(normal)
        square = jnp.sum(place * place, axis=0, keepdims=True)
        inner = -jnp.sum(place * normal, axis=0, keepdims=True)
        ones = jnp.ones((3, SPAN), f32)
        zeros = jnp.zeros((8, SPAN), f32)
        s1, s2, s3 = three_parts(square)
        i1, i2, i3 = three_parts(inner)
        feats[0:1], feats[1:2], feats[2:3] = s1, s2, s3
        feats[3:6] = ones
        for slot, part in enumerate((p1, p1, p2, p2, p1, p3)):
            feats[6 + 3 * slot : 9 + 3 * slot] = part * -2.0
        feats[24:32] = zeros
        feats[32:40] = zeros
        feats[32:33], feats[33:34], feats[34:35] = i1, i2, i3
        for slot, part in enumerate((n1, n1, n2, n2, n1, n3)):
            feats[38 + 3 * slot : 41 + 3 * slot] = part
        feats[56:64] = zeros
        for leaf in range(LEAF_DEV):
            cols = slice(LEAF * leaf, LEAF * leaf + LEAF)
            place_held = LEAF_DEV * side + leaf
            sources[place_held, :, 0:LEAF] = feats[0:FEATURES, cols].astype(bf16)
            sources[place_held, :, LEAF:] = feats[FEATURES:, cols].astype(bf16)
            dens_high, dens_low = two_parts(block[0:RHS, cols])
            dens_parts[place_held, 0:RHS, 0:LEAF] = dens_high
            dens_parts[place_held, 0:RHS, LEAF:] = dens_high
            dens_parts[place_held, RHS:, 0:LEAF] = dens_low
            dens_parts[place_held, RHS:, LEAF:] = jnp.zeros((RHS, LEAF), bf16)
        if side == 1:
            t1, t2, t3 = three_parts(square + smooth_sq)
            feats[0:3] = ones
            feats[3:4], feats[4:5], feats[5:6] = t1, t2, t3
            for slot, part in enumerate((p1, p2, p1, p2, p3, p1)):
                feats[6 + 3 * slot : 9 + 3 * slot] = part
            feats[24:32] = zeros
            for leaf in range(LEAF_DEV):
                targets[leaf] = jnp.transpose(feats[0:FEATURES, LEAF * leaf : LEAF * leaf + LEAF]).astype(bf16)

    near_t[...] = jnp.zeros((LEAF_DEV, LEAF, 2 * RHS), f32)

    def one_block(entry):
        leaf = work[0, entry]
        source = work[1, entry]
        uses = work[2, entry].astype(f32)
        both = bf16_dot(targets[leaf], sources[source])
        inverse = lax.rsqrt(both[:, :LEAF])
        block = both[:, LEAF:] * (inverse * inverse * inverse)
        high, low = two_parts(block)
        term = lax.dot_general(
            jnp.concatenate([high, low], axis=1),
            dens_parts[source],
            (((1,), (1,)), ((), ())),
            preferred_element_type=f32,
        )
        return leaf, uses * term

    def some_blocks(step, carry):
        results = [one_block(GROUP * step + k) for k in range(GROUP)]
        for leaf, term in results:
            near_t[leaf] = near_t[leaf] + term
        return carry

    lax.fori_loop(0, (count + GROUP - 1) // GROUP, some_blocks, 0)
    for leaf in range(LEAF_DEV):
        total = jnp.transpose(near_t[leaf])
        near_out[leaf] = 0.5 * own[0:RHS, LEAF * leaf : LEAF * leaf + LEAF] + total[:RHS] + total[RHS:]

    for side in range(3):
        for c in range(LEAF_DEV):
            split_leaf[LEAF_DEV * side + c] = unpack(halo[side][COEF_ROW:, 128 * c : 128 * c + 128])
        for m in range(MID_DEV):
            lanes = slice(128 * (LEAF_DEV + m), 128 * (LEAF_DEV + m) + 128)
            split_mid[MID_DEV * side + m] = unpack(halo[side][COEF_ROW:, lanes])
    for couple, number, adm, split, offset, result in (
        (couple_leaf, LEAF_DEV, adm_leaf, split_leaf, first_leaf, leaf_couple),
        (couple_mid, MID_DEV, adm_mid, split_mid, first_mid, mid_couple),
    ):
        slots = couple.shape[0]
        for a in range(slots):
            for chunk in range(CHUNKS):
                rows[a, 8 * chunk : 8 * chunk + number, :] = couple[a, :, 128 * chunk : 128 * chunk + 128]
        for t in range(number):
            lhs = jnp.concatenate([rows[a, pl.ds(t, CHUNKS, stride=8), :] for a in range(slots)], axis=0)
            rhs = jnp.concatenate([split[held(adm[t, a] - offset + number, number)] for a in range(slots)], axis=0)
            result[t] = fold(dot(lhs, rhs, 0, 0))
    for c in range(LEAF_DEV):
        cols = slice(LEAF * c, LEAF * c + LEAF)
        field = leaf_couple[c] + dot(leaf_mats[c], mid_couple[c // 2])
        base[:, cols] = near_out[c] + dot(field, row_basis[:, cols], 0, 0)


def matrix_kernel(couple_top, down_mid, down_leaf, row_basis, top_mats, leaf_mats, top_to_points, mid_mats, rows, natural):
    for chunk in range(CHUNKS):
        rows[16 * chunk : 16 * chunk + ADM_TOP, :] = couple_top[0, :, 128 * chunk : 128 * chunk + 128]
    for group in range(4):
        stack = jnp.concatenate(
            [rows[pl.ds(4 * group + a, CHUNKS, stride=16), :] for a in range(4)], axis=0
        )
        high, low = two_parts(jnp.transpose(stack))
        top_mats[0:128, 128 * group : 128 * group + 128] = high
        top_mats[128:, 128 * group : 128 * group + 128] = low
    for source, result, number in ((down_mid, mid_mats, MID_DEV), (down_leaf, leaf_mats, LEAF_DEV)):
        for chunk in range(CHUNKS):
            rows[8 * chunk : 8 * chunk + number, :] = source[:, 128 * chunk : 128 * chunk + 128]
        for c in range(number):
            wide = rows[pl.ds(c, CHUNKS, stride=8), :]
            swapped = jnp.concatenate([wide[:, RANK:], wide[:, :RANK]], axis=1)
            natural[pl.ds(0, HALF, stride=2), :] = wide
            natural[pl.ds(1, HALF, stride=2), :] = swapped
            result[c] = jnp.transpose(natural[...])[:RANK]
    for c in range(LEAF_DEV):
        cols = slice(LEAF * c, LEAF * c + LEAF)
        high, low = two_parts(dot(dot(leaf_mats[c], mid_mats[c // 2]), row_basis[:, cols], 0, 0))
        top_to_points[0:RANK, cols] = high
        top_to_points[RANK : 2 * RANK, cols] = high
        top_to_points[2 * RANK :, cols] = low


def matrix_call(*operands):
    return pl.pallas_call(
        matrix_kernel,
        name="transposed_matrices",
        out_shape=(
            jax.ShapeDtypeStruct((256, ADM_TOP * HALF), bf16),
            jax.ShapeDtypeStruct((LEAF_DEV, RANK, RANK), f32),
            jax.ShapeDtypeStruct((3 * RANK, SPAN), bf16),
        ),
        in_specs=[VMEM] * 4,
        out_specs=(VMEM,) * 3,
        scratch_shapes=[
            pltpu.VMEM((MID_DEV, RANK, RANK), f32),
            pltpu.VMEM((16 * CHUNKS, 128), f32),
            pltpu.VMEM((RANK, 128), f32),
        ],
        compiler_params=pltpu.CompilerParams(vmem_limit_bytes=VMEM_LIMIT),
        cost_estimate=pl.CostEstimate(flops=2_000_000_000, bytes_accessed=2_000_000, transcendentals=0),
    )(*operands)


def near_call(near_list, near_count, adm_leaf, adm_mid, *rest):
    return pl.pallas_call(
        near_kernel,
        name="near_and_couplings",
        out_shape=(
            jax.ShapeDtypeStruct((RHS, SPAN), f32),
            jax.ShapeDtypeStruct((4, ADM_TOP), jnp.int32),
        ),
        in_specs=[SMEM] * 4 + [VMEM] * 7 + [SMEM] * 2,
        out_specs=(VMEM, SMEM),
        scratch_shapes=[
            pltpu.VMEM((LEAF_DEV, RHS, LEAF), f32),
            pltpu.VMEM((LEAF_DEV, LEAF, 2 * RHS), f32),
            pltpu.VMEM((LEAF_DEV, RANK, RHS), f32),
            pltpu.VMEM((MID_DEV, RANK, RHS), f32),
            pltpu.VMEM((2 * FEATURES, SPAN), f32),
            pltpu.VMEM((3 * LEAF_DEV, FEATURES, 2 * LEAF), bf16),
            pltpu.VMEM((LEAF_DEV, LEAF, FEATURES), bf16),
            pltpu.VMEM((3 * LEAF_DEV, 2 * RHS, 2 * LEAF), bf16),
            pltpu.VMEM((3 * LEAF_DEV, HALF, HALF), f32),
            pltpu.VMEM((3 * MID_DEV, HALF, HALF), f32),
            pltpu.VMEM((ADM_LEAF, 8 * CHUNKS, 128), f32),
            pltpu.SMEM((3, LEAF_DEV * NEAR + 8), jnp.int32),
        ],
        compiler_params=pltpu.CompilerParams(vmem_limit_bytes=VMEM_LIMIT),
        cost_estimate=pl.CostEstimate(flops=4_000_000_000, bytes_accessed=2_000_000, transcendentals=2_000_000),
    )(near_list, near_count, adm_leaf, adm_mid, *rest)


def top_share(top_mats, chosen):
    high, low = two_parts(chosen)
    product = bf16_dot(top_mats[...], jnp.concatenate([high, low], axis=1))
    width = 2 * RHS
    return fold(product[:128, :width] + product[:128, width:] + product[128:, :width])


def held_tops(plan, row, tops):
    return [
        jnp.where(plan[row + 1, a] == 1, tops[plan[row, a]], jnp.zeros((8, 128), f32)) for a in range(ADM_TOP)
    ]


def answer_kernel(plan, own_tops, out):
    for a, tile in enumerate(held_tops(plan, 2, own_tops)):
        out[a] = tile


def answer_call(plan, own_tops):
    return pl.pallas_call(
        answer_kernel,
        name="answer",
        out_shape=jax.ShapeDtypeStruct((ADM_TOP, 8, 128), f32),
        in_specs=[SMEM, VMEM],
        out_specs=VMEM,
        compiler_params=pltpu.CompilerParams(vmem_limit_bytes=VMEM_LIMIT),
        cost_estimate=pl.CostEstimate(flops=1_000_000, bytes_accessed=100_000, transcendentals=0),
    )(plan, own_tops)


def own_kernel(plan, own_tops, top_mats, out):
    out[...] = top_share(top_mats, jnp.concatenate([unpack(tile) for tile in held_tops(plan, 0, own_tops)], axis=0))


def own_call(plan, own_tops, top_mats):
    return pl.pallas_call(
        own_kernel,
        name="own_tops",
        out_shape=jax.ShapeDtypeStruct((RANK, RHS), f32),
        in_specs=[SMEM, VMEM, VMEM],
        out_specs=VMEM,
        compiler_params=pltpu.CompilerParams(vmem_limit_bytes=VMEM_LIMIT),
        cost_estimate=pl.CostEstimate(flops=400_000_000, bytes_accessed=400_000, transcendentals=0),
    )(plan, own_tops, top_mats)


def down_kernel(received, own_share, base, top_mats, top_to_points, out):
    chosen = jnp.concatenate([unpack(received[a]) for a in range(ADM_TOP)], axis=0)
    top_field = own_share[...] + top_share(top_mats, chosen)
    high, low = two_parts(jnp.transpose(top_field))
    out[...] = base[...] + bf16_dot(jnp.concatenate([high, low, high], axis=1), top_to_points[...])


def down_call(*operands):
    return pl.pallas_call(
        down_kernel,
        name="down_sweep",
        out_shape=jax.ShapeDtypeStruct((RHS, SPAN), f32),
        in_specs=[VMEM] * 5,
        out_specs=VMEM,
        compiler_params=pltpu.CompilerParams(vmem_limit_bytes=VMEM_LIMIT),
        cost_estimate=pl.CostEstimate(flops=10_000_000, bytes_accessed=800_000, transcendentals=0),
    )(*operands)


def solution(mesh):
    devices = mesh.devices.size
    cores = 2
    ring = 16
    planes = devices // (cores * ring)
    along_z = [
        [(plane * ring + z) * cores + core for z in range(ring)] for plane in range(planes) for core in range(cores)
    ]
    across = [
        [(plane * ring + z) * cores + core for plane in range(planes)] for z in range(ring) for core in range(cores)
    ]

    def on_device(
        densities,
        points,
        area_normals,
        col_basis,
        row_basis,
        up_leaf,
        up_mid,
        down_leaf,
        down_mid,
        couple_leaf,
        couple_mid,
        couple_top,
        near_list,
        near_count,
        adm_leaf,
        adm_mid,
        adm_top,
    ):
        own_top, coefs = up_call(densities, col_basis, up_leaf, up_mid, ring)
        own_top, coefs, couple_top, down_mid, down_leaf = lax.optimization_barrier(
            (own_top, coefs, couple_top, down_mid, down_leaf)
        )
        packed = pack_call(densities, points, area_normals, coefs, adm_top)
        ring_tops = lax.all_to_all(own_top, "leaf", 0, 0, axis_index_groups=along_z, tiled=True)
        same_chip = lax.ppermute(packed, "leaf", [(i, i ^ 1) for i in range(devices)])
        next_chip = lax.ppermute(packed, "leaf", [(i, ((i + 1) ^ 1) - 1) for i in range(1, devices - 1)])
        top_mats, leaf_mats, top_to_points = matrix_call(couple_top, down_mid, down_leaf, row_basis)
        ring_tops, same_chip, next_chip, top_mats, leaf_mats, top_to_points = lax.optimization_barrier(
            (ring_tops, same_chip, next_chip, top_mats, leaf_mats, top_to_points)
        )
        spread = jnp.broadcast_to(ring_tops.reshape(1, ring * 8, 128), (planes, ring * 8, 128))
        core_tops = lax.all_to_all(spread, "leaf", 0, 0, axis_index_groups=across, tiled=True)
        wanted = same_chip[WANTED_ROW : WANTED_ROW + 1, 0:ADM_TOP].astype(jnp.int32)
        base, plan = near_call(
            near_list,
            near_count,
            adm_leaf,
            adm_mid,
            packed,
            same_chip,
            next_chip,
            jnp.swapaxes(couple_leaf, 0, 1),
            jnp.swapaxes(couple_mid, 0, 1),
            leaf_mats,
            row_basis,
            adm_top,
            wanted,
        )
        core_tops, base, plan = lax.optimization_barrier((core_tops, base, plan))
        core_tops = core_tops.reshape(planes * ring, 8, 128)
        answers = answer_call(plan, core_tops)
        received = lax.ppermute(answers, "leaf", [(i, i ^ 1) for i in range(devices)])
        answers, plan, core_tops = lax.optimization_barrier((answers, plan, core_tops))
        own_share = own_call(plan, core_tops, top_mats)
        return down_call(
            received,
            own_share,
            base,
            top_mats,
            top_to_points,
        )

    split_last = P(None, "leaf")
    split_first = P("leaf", None)
    split_three = P("leaf", None, None)
    return jax.shard_map(
        on_device,
        mesh=mesh,
        in_specs=(split_last,) * 5
        + (split_first,) * 4
        + (split_three,) * 3
        + (split_first, P("leaf"), split_first, split_first, split_first),
        out_specs=split_last,
        check_vma=False,
    )
```

```python
import math

import jax
import jax.numpy as jnp
from jax import lax
from jax.experimental import pallas as pl
from jax.experimental.pallas import tpu as pltpu
from jax.sharding import PartitionSpec as P

RHS = 16
LEAF = 256
RANK = 64
HALF = RANK // 2
LEAF_DEV = 4
MID_DEV = 2
NEAR = 8
ADM_LEAF = 6
ADM_MID = 6
ADM_TOP = 16
SPAN = LEAF_DEV * LEAF
CHUNKS = RANK * RANK // 128
FEATURES = 32
PACKED_ROWS = 32
WANTED_ROW = 22
COEF_ROW = 24
GROUP = 8
VMEM_LIMIT = 16 * 1024 * 1024
CORES = 2
RING = 16
PLANES = 16
FIRST_Z = 11
FIRST_PLANE = 10

smooth_sq = 0.01
four_pi = 4.0 * math.pi
highest = lax.Precision.HIGHEST
f32 = jnp.float32
bf16 = jnp.bfloat16

SMEM = pl.BlockSpec(memory_space=pltpu.SMEM)
VMEM = pl.BlockSpec(memory_space=pltpu.VMEM)


def dot(lhs, rhs, lhs_dim=1, rhs_dim=0):
    return lax.dot_general(
        lhs,
        rhs,
        (((lhs_dim,), (rhs_dim,)), ((), ())),
        precision=highest,
        preferred_element_type=f32,
    )


def even_odd(ref, index):
    even = ref[index, pl.ds(0, HALF, stride=2), :]
    odd = ref[index, pl.ds(1, HALF, stride=2), :]
    return jnp.concatenate([even[:, :RHS], odd[:, :RHS]], axis=1)


def pack(split):
    return jnp.concatenate([split[8 * g : 8 * g + 8] for g in range(4)], axis=1)


def unpack(tile):
    return jnp.concatenate([tile[:, 32 * g : 32 * g + 32] for g in range(4)], axis=0)


def fold(product):
    return product[:RANK, :RHS] + product[RANK:, RHS:]


def dot_parts(lhs, rhs, lhs_dim=1, rhs_dim=0):
    lhs_high, lhs_low = two_parts(lhs)
    rhs_high, rhs_low = two_parts(rhs)
    return lax.dot_general(
        jnp.concatenate([lhs_high, lhs_high, lhs_low], axis=lhs_dim),
        jnp.concatenate([rhs_high, rhs_low, rhs_high], axis=rhs_dim),
        (((lhs_dim,), (rhs_dim,)), ((), ())),
        preferred_element_type=f32,
    )


def up_kernel(dens, col_basis, up_leaf, up_mid, top_out, coefs, leaf_rows, mid_rows, leaf_t, mid_t):
    for chunk in range(CHUNKS):
        lanes = slice(128 * chunk, 128 * chunk + 128)
        leaf_rows[8 * chunk : 8 * chunk + LEAF_DEV, :] = up_leaf[:, lanes]
        mid_rows[8 * chunk : 8 * chunk + MID_DEV, :] = up_mid[:, lanes]
    for c in range(LEAF_DEV):
        cols = slice(LEAF * c, LEAF * c + LEAF)
        leaf_t[c, :, 0:RHS] = dot_parts(col_basis[:, cols], dens[:, cols], 1, 1)
    leaf_split = [even_odd(leaf_t, c) for c in range(LEAF_DEV)]
    for c in range(LEAF_DEV):
        coefs[:, 128 * c : 128 * c + 128] = pack(leaf_split[c])
    for m in range(MID_DEV):
        pair = (2 * m, 2 * m + 1)
        lhs = jnp.concatenate([leaf_rows[pl.ds(c, CHUNKS, stride=8), :] for c in pair], axis=0)
        rhs = jnp.concatenate([leaf_split[c] for c in pair], axis=0)
        mid_t[m, :, 0:RHS] = fold(dot_parts(lhs, rhs, 0, 0))
    mid_split = [even_odd(mid_t, m) for m in range(MID_DEV)]
    for m in range(MID_DEV):
        coefs[:, 128 * (LEAF_DEV + m) : 128 * (LEAF_DEV + m) + 128] = pack(mid_split[m])
    lhs = jnp.concatenate([mid_rows[pl.ds(m, CHUNKS, stride=8), :] for m in range(MID_DEV)], axis=0)
    rhs = jnp.concatenate(mid_split, axis=0)
    leaf_t[0, :, 0:RHS] = fold(dot_parts(lhs, rhs, 0, 0))
    tile = pack(even_odd(leaf_t, 0))
    for peer in range(top_out.shape[0]):
        top_out[peer] = tile


def pack_kernel(dens, points, normals, coefs, adm_top, packed):
    packed[0:RHS, :] = dens[...]
    packed[RHS : RHS + 3, :] = points[...]
    packed[RHS + 3 : RHS + 6, :] = normals[...]
    packed[WANTED_ROW:COEF_ROW, :] = jnp.zeros((COEF_ROW - WANTED_ROW, SPAN), f32)
    packed[WANTED_ROW : WANTED_ROW + 1, 0:ADM_TOP] = adm_top[...].astype(f32)
    packed[COEF_ROW:, 0 : 6 * 128] = coefs[...]
    packed[COEF_ROW:, 6 * 128 :] = jnp.zeros((8, SPAN - 6 * 128), f32)


def pack_call(*operands):
    return pl.pallas_call(
        pack_kernel,
        name="packed_for_neighbours",
        out_shape=jax.ShapeDtypeStruct((PACKED_ROWS, SPAN), f32),
        in_specs=[VMEM] * 5,
        out_specs=VMEM,
        compiler_params=pltpu.CompilerParams(vmem_limit_bytes=VMEM_LIMIT),
        cost_estimate=pl.CostEstimate(flops=100_000_000, bytes_accessed=400_000, transcendentals=0),
    )(*operands)


def up_call(dens, col_basis, up_leaf, up_mid, peers):
    return pl.pallas_call(
        up_kernel,
        name="up_sweep",
        out_shape=(
            jax.ShapeDtypeStruct((peers, 8, 128), f32),
            jax.ShapeDtypeStruct((8, 6 * 128), f32),
        ),
        in_specs=[VMEM] * 4,
        out_specs=(VMEM, VMEM),
        scratch_shapes=[
            pltpu.VMEM((8 * CHUNKS, 128), f32),
            pltpu.VMEM((8 * CHUNKS, 128), f32),
            pltpu.VMEM((LEAF_DEV, RANK, 128), f32),
            pltpu.VMEM((MID_DEV, RANK, 128), f32),
        ],
        cost_estimate=pl.CostEstimate(flops=10_000_000, bytes_accessed=800_000, transcendentals=0),
    )(dens, col_basis, up_leaf, up_mid)


def two_parts(values):
    first = values.astype(bf16)
    return first, (values - first.astype(f32)).astype(bf16)


def bf16_dot(lhs, rhs):
    return lax.dot_general(lhs, rhs, (((1,), (0,)), ((), ())), preferred_element_type=f32)


def three_parts(values):
    first = values.astype(bf16).astype(f32)
    rest = values - first
    second = rest.astype(bf16).astype(f32)
    return first, second, (rest - second).astype(bf16).astype(f32)


def near_kernel(
    near_list,
    near_count,
    adm_leaf,
    adm_mid,
    own,
    same_chip,
    next_chip,
    couple_leaf,
    couple_mid,
    leaf_mats,
    row_basis,
    adm_top,
    wanted,
    base,
    plan,
    near_out,
    near_t,
    leaf_couple,
    mid_couple,
    feats,
    sources,
    targets,
    dens_parts,
    split_leaf,
    split_mid,
    rows,
    work,
):
    halo = (same_chip, own, next_chip)
    first_leaf = near_list[0, 0]
    first_mid = first_leaf // 2
    core = (first_leaf // LEAF_DEV) % 2

    def held(place, number):
        side = place // number
        return jnp.where(core == 0, place + (2 - 2 * side) * number, place)

    for row, tops in ((0, adm_top), (2, wanted)):
        for a in range(ADM_TOP):
            plane = tops[0, a] // (CORES * RING)
            z = tops[0, a] // CORES % RING
            plan[row, a] = (plane + PLANES - FIRST_PLANE) % PLANES * RING + (z + RING - FIRST_Z) % RING
            plan[row + 1, a] = (tops[0, a] % CORES == core).astype(jnp.int32)

    count = jnp.int32(0)
    for i in range(LEAF_DEV):
        limit = near_count[i]
        slots = [near_list[i, j] for j in range(NEAR)]
        used = [jnp.int32(j) < limit for j in range(NEAR)]
        for j in range(NEAR):
            uses = jnp.int32(0)
            fresh = used[j]
            for other in range(NEAR):
                same = jnp.logical_and(used[other], slots[other] == slots[j])
                uses = uses + same.astype(jnp.int32)
                if other < j:
                    fresh = jnp.logical_and(fresh, jnp.logical_not(same))
            work[0, count] = jnp.int32(i)
            work[1, count] = held(slots[j] - first_leaf + LEAF_DEV, LEAF_DEV)
            work[2, count] = uses
            count = count + fresh.astype(jnp.int32)
    for extra in range(GROUP):
        work[0, count + extra] = jnp.int32(0)
        work[1, count + extra] = jnp.int32(0)
        work[2, count + extra] = jnp.int32(0)

    for side in range(3):
        block = halo[side]
        place = block[RHS : RHS + 3, :] - 0.5
        normal = block[RHS + 3 : RHS + 6, :] * (1.0 / four_pi)
        p1, p2, p3 = three_parts(place)
        n1, n2, n3 = three_parts(normal)
        square = jnp.sum(place * place, axis=0, keepdims=True)
        inner = -jnp.sum(place * normal, axis=0, keepdims=True)
        ones = jnp.ones((3, SPAN), f32)
        zeros = jnp.zeros((8, SPAN), f32)
        s1, s2, s3 = three_parts(square)
        i1, i2, i3 = three_parts(inner)
        feats[0:1], feats[1:2], feats[2:3] = s1, s2, s3
        feats[3:6] = ones
        for slot, part in enumerate((p1, p1, p2, p2, p1, p3)):
            feats[6 + 3 * slot : 9 + 3 * slot] = part * -2.0
        feats[24:32] = zeros
        feats[32:40] = zeros
        feats[32:33], feats[33:34], feats[34:35] = i1, i2, i3
        for slot, part in enumerate((n1, n1, n2, n2, n1, n3)):
            feats[38 + 3 * slot : 41 + 3 * slot] = part
        feats[56:64] = zeros
        for leaf in range(LEAF_DEV):
            cols = slice(LEAF * leaf, LEAF * leaf + LEAF)
            place_held = LEAF_DEV * side + leaf
            sources[place_held, :, 0:LEAF] = feats[0:FEATURES, cols].astype(bf16)
            sources[place_held, :, LEAF:] = feats[FEATURES:, cols].astype(bf16)
            dens_high, dens_low = two_parts(block[0:RHS, cols])
            dens_parts[place_held, 0:RHS, 0:LEAF] = dens_high
            dens_parts[place_held, 0:RHS, LEAF:] = dens_high
            dens_parts[place_held, RHS:, 0:LEAF] = dens_low
            dens_parts[place_held, RHS:, LEAF:] = jnp.zeros((RHS, LEAF), bf16)
        if side == 1:
            t1, t2, t3 = three_parts(square + smooth_sq)
            feats[0:3] = ones
            feats[3:4], feats[4:5], feats[5:6] = t1, t2, t3
            for slot, part in enumerate((p1, p2, p1, p2, p3, p1)):
                feats[6 + 3 * slot : 9 + 3 * slot] = part
            feats[24:32] = zeros
            for leaf in range(LEAF_DEV):
                targets[leaf] = jnp.transpose(feats[0:FEATURES, LEAF * leaf : LEAF * leaf + LEAF]).astype(bf16)

    near_t[...] = jnp.zeros((LEAF_DEV, LEAF, 2 * RHS), f32)

    def one_block(entry):
        leaf = work[0, entry]
        source = work[1, entry]
        uses = work[2, entry].astype(f32)
        both = bf16_dot(targets[leaf], sources[source])
        inverse = lax.rsqrt(both[:, :LEAF])
        block = both[:, LEAF:] * (inverse * inverse * inverse)
        high, low = two_parts(block)
        term = lax.dot_general(
            jnp.concatenate([high, low], axis=1),
            dens_parts[source],
            (((1,), (1,)), ((), ())),
            preferred_element_type=f32,
        )
        return leaf, uses * term

    def some_blocks(step, carry):
        results = [one_block(GROUP * step + k) for k in range(GROUP)]
        for leaf, term in results:
            near_t[leaf] = near_t[leaf] + term
        return carry

    lax.fori_loop(0, (count + GROUP - 1) // GROUP, some_blocks, 0)
    for leaf in range(LEAF_DEV):
        total = jnp.transpose(near_t[leaf])
        near_out[leaf] = 0.5 * own[0:RHS, LEAF * leaf : LEAF * leaf + LEAF] + total[:RHS] + total[RHS:]

    for side in range(3):
        for c in range(LEAF_DEV):
            split_leaf[LEAF_DEV * side + c] = unpack(halo[side][COEF_ROW:, 128 * c : 128 * c + 128])
        for m in range(MID_DEV):
            lanes = slice(128 * (LEAF_DEV + m), 128 * (LEAF_DEV + m) + 128)
            split_mid[MID_DEV * side + m] = unpack(halo[side][COEF_ROW:, lanes])
    for couple, number, adm, split, offset, result in (
        (couple_leaf, LEAF_DEV, adm_leaf, split_leaf, first_leaf, leaf_couple),
        (couple_mid, MID_DEV, adm_mid, split_mid, first_mid, mid_couple),
    ):
        slots = couple.shape[0]
        for a in range(slots):
            for chunk in range(CHUNKS):
                rows[a, 8 * chunk : 8 * chunk + number, :] = couple[a, :, 128 * chunk : 128 * chunk + 128]
        for t in range(number):
            lhs = jnp.concatenate([rows[a, pl.ds(t, CHUNKS, stride=8), :] for a in range(slots)], axis=0)
            rhs = jnp.concatenate([split[held(adm[t, a] - offset + number, number)] for a in range(slots)], axis=0)
            result[t] = fold(dot(lhs, rhs, 0, 0))
    for c in range(LEAF_DEV):
        cols = slice(LEAF * c, LEAF * c + LEAF)
        field = leaf_couple[c] + dot(leaf_mats[c], mid_couple[c // 2])
        base[:, cols] = near_out[c] + dot(field, row_basis[:, cols], 0, 0)


def matrix_kernel(couple_top, down_mid, down_leaf, row_basis, top_mats, leaf_mats, top_to_points, mid_mats, rows, natural):
    for chunk in range(CHUNKS):
        rows[16 * chunk : 16 * chunk + ADM_TOP, :] = couple_top[0, :, 128 * chunk : 128 * chunk + 128]
    for group in range(4):
        stack = jnp.concatenate(
            [rows[pl.ds(4 * group + a, CHUNKS, stride=16), :] for a in range(4)], axis=0
        )
        high, low = two_parts(jnp.transpose(stack))
        top_mats[0:128, 128 * group : 128 * group + 128] = high
        top_mats[128:, 128 * group : 128 * group + 128] = low
    for source, result, number in ((down_mid, mid_mats, MID_DEV), (down_leaf, leaf_mats, LEAF_DEV)):
        for chunk in range(CHUNKS):
            rows[8 * chunk : 8 * chunk + number, :] = source[:, 128 * chunk : 128 * chunk + 128]
        for c in range(number):
            wide = rows[pl.ds(c, CHUNKS, stride=8), :]
            swapped = jnp.concatenate([wide[:, RANK:], wide[:, :RANK]], axis=1)
            natural[pl.ds(0, HALF, stride=2), :] = wide
            natural[pl.ds(1, HALF, stride=2), :] = swapped
            result[c] = jnp.transpose(natural[...])[:RANK]
    for c in range(LEAF_DEV):
        cols = slice(LEAF * c, LEAF * c + LEAF)
        high, low = two_parts(dot(dot(leaf_mats[c], mid_mats[c // 2]), row_basis[:, cols], 0, 0))
        top_to_points[0:RANK, cols] = high
        top_to_points[RANK : 2 * RANK, cols] = high
        top_to_points[2 * RANK :, cols] = low


def matrix_call(*operands):
    return pl.pallas_call(
        matrix_kernel,
        name="transposed_matrices",
        out_shape=(
            jax.ShapeDtypeStruct((256, ADM_TOP * HALF), bf16),
            jax.ShapeDtypeStruct((LEAF_DEV, RANK, RANK), f32),
            jax.ShapeDtypeStruct((3 * RANK, SPAN), bf16),
        ),
        in_specs=[VMEM] * 4,
        out_specs=(VMEM,) * 3,
        scratch_shapes=[
            pltpu.VMEM((MID_DEV, RANK, RANK), f32),
            pltpu.VMEM((16 * CHUNKS, 128), f32),
            pltpu.VMEM((RANK, 128), f32),
        ],
        compiler_params=pltpu.CompilerParams(vmem_limit_bytes=VMEM_LIMIT),
        cost_estimate=pl.CostEstimate(flops=2_000_000_000, bytes_accessed=2_000_000, transcendentals=0),
    )(*operands)


def near_call(near_list, near_count, adm_leaf, adm_mid, *rest):
    return pl.pallas_call(
        near_kernel,
        name="near_and_couplings",
        out_shape=(
            jax.ShapeDtypeStruct((RHS, SPAN), f32),
            jax.ShapeDtypeStruct((4, ADM_TOP), jnp.int32),
        ),
        in_specs=[SMEM] * 4 + [VMEM] * 7 + [SMEM] * 2,
        out_specs=(VMEM, SMEM),
        scratch_shapes=[
            pltpu.VMEM((LEAF_DEV, RHS, LEAF), f32),
            pltpu.VMEM((LEAF_DEV, LEAF, 2 * RHS), f32),
            pltpu.VMEM((LEAF_DEV, RANK, RHS), f32),
            pltpu.VMEM((MID_DEV, RANK, RHS), f32),
            pltpu.VMEM((2 * FEATURES, SPAN), f32),
            pltpu.VMEM((3 * LEAF_DEV, FEATURES, 2 * LEAF), bf16),
            pltpu.VMEM((LEAF_DEV, LEAF, FEATURES), bf16),
            pltpu.VMEM((3 * LEAF_DEV, 2 * RHS, 2 * LEAF), bf16),
            pltpu.VMEM((3 * LEAF_DEV, HALF, HALF), f32),
            pltpu.VMEM((3 * MID_DEV, HALF, HALF), f32),
            pltpu.VMEM((ADM_LEAF, 8 * CHUNKS, 128), f32),
            pltpu.SMEM((3, LEAF_DEV * NEAR + 8), jnp.int32),
        ],
        compiler_params=pltpu.CompilerParams(vmem_limit_bytes=VMEM_LIMIT),
        cost_estimate=pl.CostEstimate(flops=4_000_000_000, bytes_accessed=2_000_000, transcendentals=2_000_000),
    )(near_list, near_count, adm_leaf, adm_mid, *rest)


def top_share(top_mats, chosen):
    high, low = two_parts(chosen)
    product = bf16_dot(top_mats[...], jnp.concatenate([high, low], axis=1))
    width = 2 * RHS
    return fold(product[:128, :width] + product[:128, width:] + product[128:, :width])


def held_tops(plan, row, tops):
    return [
        jnp.where(plan[row + 1, a] == 1, tops[plan[row, a]], jnp.zeros((8, 128), f32)) for a in range(ADM_TOP)
    ]


def answer_kernel(plan, own_tops, out):
    for a, tile in enumerate(held_tops(plan, 2, own_tops)):
        out[a] = tile


def answer_call(plan, own_tops):
    return pl.pallas_call(
        answer_kernel,
        name="answer",
        out_shape=jax.ShapeDtypeStruct((ADM_TOP, 8, 128), f32),
        in_specs=[SMEM, VMEM],
        out_specs=VMEM,
        compiler_params=pltpu.CompilerParams(vmem_limit_bytes=VMEM_LIMIT),
        cost_estimate=pl.CostEstimate(flops=1_000_000, bytes_accessed=100_000, transcendentals=0),
    )(plan, own_tops)


def own_kernel(plan, own_tops, top_mats, out):
    out[...] = top_share(top_mats, jnp.concatenate([unpack(tile) for tile in held_tops(plan, 0, own_tops)], axis=0))


def own_call(plan, own_tops, top_mats):
    return pl.pallas_call(
        own_kernel,
        name="own_tops",
        out_shape=jax.ShapeDtypeStruct((RANK, RHS), f32),
        in_specs=[SMEM, VMEM, VMEM],
        out_specs=VMEM,
        compiler_params=pltpu.CompilerParams(vmem_limit_bytes=VMEM_LIMIT),
        cost_estimate=pl.CostEstimate(flops=400_000_000, bytes_accessed=400_000, transcendentals=0),
    )(plan, own_tops, top_mats)


def down_kernel(received, own_share, base, top_mats, top_to_points, out):
    chosen = jnp.concatenate([unpack(received[a]) for a in range(ADM_TOP)], axis=0)
    top_field = own_share[...] + top_share(top_mats, chosen)
    high, low = two_parts(jnp.transpose(top_field))
    out[...] = base[...] + bf16_dot(jnp.concatenate([high, low, high], axis=1), top_to_points[...])


def down_call(*operands):
    return pl.pallas_call(
        down_kernel,
        name="down_sweep",
        out_shape=jax.ShapeDtypeStruct((RHS, SPAN), f32),
        in_specs=[VMEM] * 5,
        out_specs=VMEM,
        compiler_params=pltpu.CompilerParams(vmem_limit_bytes=VMEM_LIMIT),
        cost_estimate=pl.CostEstimate(flops=10_000_000, bytes_accessed=800_000, transcendentals=0),
    )(*operands)


def solution(mesh):
    devices = mesh.devices.size
    ring = [(FIRST_Z + i) % RING for i in range(RING)]
    planes = [(FIRST_PLANE + i) % PLANES for i in range(PLANES)]
    along_z = [[(p * RING + z) * CORES + c for z in ring] for p in range(PLANES) for c in range(CORES)]
    across = [[(p * RING + z) * CORES + c for p in planes] for z in range(RING) for c in range(CORES)]

    def on_device(
        densities,
        points,
        area_normals,
        col_basis,
        row_basis,
        up_leaf,
        up_mid,
        down_leaf,
        down_mid,
        couple_leaf,
        couple_mid,
        couple_top,
        near_list,
        near_count,
        adm_leaf,
        adm_mid,
        adm_top,
    ):
        own_top, coefs = up_call(densities, col_basis, up_leaf, up_mid, RING)
        own_top, coefs, couple_top, down_mid, down_leaf = lax.optimization_barrier(
            (own_top, coefs, couple_top, down_mid, down_leaf)
        )
        packed = pack_call(densities, points, area_normals, coefs, adm_top)
        ring_tops = lax.all_to_all(own_top, "leaf", 0, 0, axis_index_groups=along_z, tiled=True)
        same_chip = lax.ppermute(packed, "leaf", [(i, i ^ 1) for i in range(devices)])
        next_chip = lax.ppermute(packed, "leaf", [(i, ((i + 1) ^ 1) - 1) for i in range(1, devices - 1)])
        top_mats, leaf_mats, top_to_points = matrix_call(couple_top, down_mid, down_leaf, row_basis)
        ring_tops, same_chip, next_chip, top_mats, leaf_mats, top_to_points = lax.optimization_barrier(
            (ring_tops, same_chip, next_chip, top_mats, leaf_mats, top_to_points)
        )
        spread = jnp.broadcast_to(ring_tops.reshape(1, RING * 8, 128), (PLANES, RING * 8, 128))
        core_tops = lax.all_to_all(spread, "leaf", 0, 0, axis_index_groups=across, tiled=True)
        wanted = same_chip[WANTED_ROW : WANTED_ROW + 1, 0:ADM_TOP].astype(jnp.int32)
        base, plan = near_call(
            near_list,
            near_count,
            adm_leaf,
            adm_mid,
            packed,
            same_chip,
            next_chip,
            jnp.swapaxes(couple_leaf, 0, 1),
            jnp.swapaxes(couple_mid, 0, 1),
            leaf_mats,
            row_basis,
            adm_top,
            wanted,
        )
        core_tops, base, plan = lax.optimization_barrier((core_tops, base, plan))
        core_tops = core_tops.reshape(PLANES * RING, 8, 128)
        answers = answer_call(plan, core_tops)
        received = lax.ppermute(answers, "leaf", [(i, i ^ 1) for i in range(devices)])
        answers, plan, core_tops = lax.optimization_barrier((answers, plan, core_tops))
        own_share = own_call(plan, core_tops, top_mats)
        return down_call(
            received,
            own_share,
            base,
            top_mats,
            top_to_points,
        )

    split_last = P(None, "leaf")
    split_first = P("leaf", None)
    split_three = P("leaf", None, None)
    return jax.shard_map(
        on_device,
        mesh=mesh,
        in_specs=(split_last,) * 5
        + (split_first,) * 4
        + (split_three,) * 3
        + (split_first, P("leaf"), split_first, split_first, split_first),
        out_specs=split_last,
        check_vma=False,
    )
```

```python
import math

import jax
import jax.numpy as jnp
from jax import lax
from jax.experimental import pallas as pl
from jax.experimental.pallas import tpu as pltpu
from jax.sharding import PartitionSpec as P

RHS = 16
LEAF = 256
RANK = 64
HALF = RANK // 2
LEAF_DEV = 4
MID_DEV = 2
NEAR = 8
ADM_LEAF = 6
ADM_MID = 6
ADM_TOP = 16
SPAN = LEAF_DEV * LEAF
CHUNKS = RANK * RANK // 128
FEATURES = 32
PACKED_ROWS = 32
WANTED_ROW = 22
COEF_ROW = 24
GROUP = 8
VMEM_LIMIT = 16 * 1024 * 1024
CORES = 2
RING = 16
PLANES = 16
FIRST_Z = 11
FIRST_PLANE = 10

smooth_sq = 0.01
four_pi = 4.0 * math.pi
highest = lax.Precision.HIGHEST
f32 = jnp.float32
bf16 = jnp.bfloat16

SMEM = pl.BlockSpec(memory_space=pltpu.SMEM)
VMEM = pl.BlockSpec(memory_space=pltpu.VMEM)


def dot(lhs, rhs, lhs_dim=1, rhs_dim=0):
    return lax.dot_general(
        lhs,
        rhs,
        (((lhs_dim,), (rhs_dim,)), ((), ())),
        precision=highest,
        preferred_element_type=f32,
    )


def even_odd(ref, index):
    even = ref[index, pl.ds(0, HALF, stride=2), :]
    odd = ref[index, pl.ds(1, HALF, stride=2), :]
    return jnp.concatenate([even[:, :RHS], odd[:, :RHS]], axis=1)


def pack(split):
    return jnp.concatenate([split[8 * g : 8 * g + 8] for g in range(4)], axis=1)


def unpack(tile):
    return jnp.concatenate([tile[:, 32 * g : 32 * g + 32] for g in range(4)], axis=0)


def fold(product):
    return product[:RANK, :RHS] + product[RANK:, RHS:]


def dot_parts(lhs, rhs, lhs_dim=1, rhs_dim=0):
    lhs_high, lhs_low = two_parts(lhs)
    rhs_high, rhs_low = two_parts(rhs)
    return lax.dot_general(
        jnp.concatenate([lhs_high, lhs_high, lhs_low], axis=lhs_dim),
        jnp.concatenate([rhs_high, rhs_low, rhs_high], axis=rhs_dim),
        (((lhs_dim,), (rhs_dim,)), ((), ())),
        preferred_element_type=f32,
    )


def up_kernel(dens, col_basis, up_leaf, up_mid, top_out, coefs, leaf_rows, mid_rows, leaf_t, mid_t):
    for chunk in range(CHUNKS):
        lanes = slice(128 * chunk, 128 * chunk + 128)
        leaf_rows[8 * chunk : 8 * chunk + LEAF_DEV, :] = up_leaf[:, lanes]
        mid_rows[8 * chunk : 8 * chunk + MID_DEV, :] = up_mid[:, lanes]
    for c in range(LEAF_DEV):
        cols = slice(LEAF * c, LEAF * c + LEAF)
        leaf_t[c, :, 0:RHS] = dot_parts(col_basis[:, cols], dens[:, cols], 1, 1)
    leaf_split = [even_odd(leaf_t, c) for c in range(LEAF_DEV)]
    for c in range(LEAF_DEV):
        coefs[:, 128 * c : 128 * c + 128] = pack(leaf_split[c])
    for m in range(MID_DEV):
        pair = (2 * m, 2 * m + 1)
        lhs = jnp.concatenate([leaf_rows[pl.ds(c, CHUNKS, stride=8), :] for c in pair], axis=0)
        rhs = jnp.concatenate([leaf_split[c] for c in pair], axis=0)
        mid_t[m, :, 0:RHS] = fold(dot_parts(lhs, rhs, 0, 0))
    mid_split = [even_odd(mid_t, m) for m in range(MID_DEV)]
    for m in range(MID_DEV):
        coefs[:, 128 * (LEAF_DEV + m) : 128 * (LEAF_DEV + m) + 128] = pack(mid_split[m])
    lhs = jnp.concatenate([mid_rows[pl.ds(m, CHUNKS, stride=8), :] for m in range(MID_DEV)], axis=0)
    rhs = jnp.concatenate(mid_split, axis=0)
    leaf_t[0, :, 0:RHS] = fold(dot_parts(lhs, rhs, 0, 0))
    tile = pack(even_odd(leaf_t, 0))
    for peer in range(top_out.shape[0]):
        top_out[peer] = tile


def pack_kernel(dens, points, normals, coefs, adm_top, packed):
    packed[0:RHS, :] = dens[...]
    packed[RHS : RHS + 3, :] = points[...]
    packed[RHS + 3 : RHS + 6, :] = normals[...]
    packed[WANTED_ROW:COEF_ROW, :] = jnp.zeros((COEF_ROW - WANTED_ROW, SPAN), f32)
    packed[WANTED_ROW : WANTED_ROW + 1, 0:ADM_TOP] = adm_top[...].astype(f32)
    packed[COEF_ROW:, 0 : 6 * 128] = coefs[...]
    packed[COEF_ROW:, 6 * 128 :] = jnp.zeros((8, SPAN - 6 * 128), f32)


def pack_call(*operands):
    return pl.pallas_call(
        pack_kernel,
        name="packed_for_neighbours",
        out_shape=jax.ShapeDtypeStruct((PACKED_ROWS, SPAN), f32),
        in_specs=[VMEM] * 5,
        out_specs=VMEM,
        compiler_params=pltpu.CompilerParams(vmem_limit_bytes=VMEM_LIMIT),
        cost_estimate=pl.CostEstimate(flops=100_000_000, bytes_accessed=400_000, transcendentals=0),
    )(*operands)


def up_call(dens, col_basis, up_leaf, up_mid, peers):
    return pl.pallas_call(
        up_kernel,
        name="up_sweep",
        out_shape=(
            jax.ShapeDtypeStruct((peers, 8, 128), f32),
            jax.ShapeDtypeStruct((8, 6 * 128), f32),
        ),
        in_specs=[VMEM] * 4,
        out_specs=(VMEM, VMEM),
        scratch_shapes=[
            pltpu.VMEM((8 * CHUNKS, 128), f32),
            pltpu.VMEM((8 * CHUNKS, 128), f32),
            pltpu.VMEM((LEAF_DEV, RANK, 128), f32),
            pltpu.VMEM((MID_DEV, RANK, 128), f32),
        ],
        cost_estimate=pl.CostEstimate(flops=10_000_000, bytes_accessed=800_000, transcendentals=0),
    )(dens, col_basis, up_leaf, up_mid)


def two_parts(values):
    first = values.astype(bf16)
    return first, (values - first.astype(f32)).astype(bf16)


def bf16_dot(lhs, rhs):
    return lax.dot_general(lhs, rhs, (((1,), (0,)), ((), ())), preferred_element_type=f32)


def three_parts(values):
    first = values.astype(bf16).astype(f32)
    rest = values - first
    second = rest.astype(bf16).astype(f32)
    return first, second, (rest - second).astype(bf16).astype(f32)


def near_kernel(
    near_list,
    near_count,
    adm_leaf,
    adm_mid,
    own,
    same_chip,
    next_chip,
    couple_leaf,
    couple_mid,
    leaf_mats,
    row_basis,
    adm_top,
    wanted,
    base,
    plan,
    near_out,
    near_t,
    leaf_couple,
    mid_couple,
    feats,
    sources,
    targets,
    dens_parts,
    split_leaf,
    split_mid,
    rows,
    work,
):
    halo = (same_chip, own, next_chip)
    first_leaf = near_list[0, 0]
    first_mid = first_leaf // 2
    core = (first_leaf // LEAF_DEV) % 2

    def held(place, number):
        side = place // number
        return jnp.where(core == 0, place + (2 - 2 * side) * number, place)

    for row, tops in ((0, adm_top), (2, wanted)):
        for a in range(ADM_TOP):
            plane = tops[0, a] // (CORES * RING)
            z = tops[0, a] // CORES % RING
            plan[row, a] = (plane + PLANES - FIRST_PLANE) % PLANES * RING + (z + RING - FIRST_Z) % RING
            plan[row + 1, a] = (tops[0, a] % CORES == core).astype(jnp.int32)

    count = jnp.int32(0)
    for i in range(LEAF_DEV):
        limit = near_count[i]
        slots = [near_list[i, j] for j in range(NEAR)]
        used = [jnp.int32(j) < limit for j in range(NEAR)]
        for j in range(NEAR):
            uses = jnp.int32(0)
            fresh = used[j]
            for other in range(NEAR):
                same = jnp.logical_and(used[other], slots[other] == slots[j])
                uses = uses + same.astype(jnp.int32)
                if other < j:
                    fresh = jnp.logical_and(fresh, jnp.logical_not(same))
            work[0, count] = jnp.int32(i)
            work[1, count] = held(slots[j] - first_leaf + LEAF_DEV, LEAF_DEV)
            work[2, count] = uses
            count = count + fresh.astype(jnp.int32)
    for extra in range(GROUP):
        work[0, count + extra] = jnp.int32(0)
        work[1, count + extra] = jnp.int32(0)
        work[2, count + extra] = jnp.int32(0)

    for side in range(3):
        block = halo[side]
        place = block[RHS : RHS + 3, :] - 0.5
        normal = block[RHS + 3 : RHS + 6, :] * (1.0 / four_pi)
        p1, p2, p3 = three_parts(place)
        n1, n2, n3 = three_parts(normal)
        square = jnp.sum(place * place, axis=0, keepdims=True)
        inner = -jnp.sum(place * normal, axis=0, keepdims=True)
        ones = jnp.ones((3, SPAN), f32)
        zeros = jnp.zeros((8, SPAN), f32)
        s1, s2, s3 = three_parts(square)
        i1, i2, i3 = three_parts(inner)
        feats[0:1], feats[1:2], feats[2:3] = s1, s2, s3
        feats[3:6] = ones
        for slot, part in enumerate((p1, p1, p2, p2, p1, p3)):
            feats[6 + 3 * slot : 9 + 3 * slot] = part * -2.0
        feats[24:32] = zeros
        feats[32:40] = zeros
        feats[32:33], feats[33:34], feats[34:35] = i1, i2, i3
        for slot, part in enumerate((n1, n1, n2, n2, n1, n3)):
            feats[38 + 3 * slot : 41 + 3 * slot] = part
        feats[56:64] = zeros
        for leaf in range(LEAF_DEV):
            cols = slice(LEAF * leaf, LEAF * leaf + LEAF)
            place_held = LEAF_DEV * side + leaf
            sources[place_held, :, 0:LEAF] = feats[0:FEATURES, cols].astype(bf16)
            sources[place_held, :, LEAF:] = feats[FEATURES:, cols].astype(bf16)
            dens_high, dens_low = two_parts(block[0:RHS, cols])
            dens_parts[place_held, 0:RHS, 0:LEAF] = dens_high
            dens_parts[place_held, 0:RHS, LEAF:] = dens_high
            dens_parts[place_held, RHS:, 0:LEAF] = dens_low
            dens_parts[place_held, RHS:, LEAF:] = jnp.zeros((RHS, LEAF), bf16)
        if side == 1:
            t1, t2, t3 = three_parts(square + smooth_sq)
            feats[0:3] = ones
            feats[3:4], feats[4:5], feats[5:6] = t1, t2, t3
            for slot, part in enumerate((p1, p2, p1, p2, p3, p1)):
                feats[6 + 3 * slot : 9 + 3 * slot] = part
            feats[24:32] = zeros
            for leaf in range(LEAF_DEV):
                targets[leaf] = jnp.transpose(feats[0:FEATURES, LEAF * leaf : LEAF * leaf + LEAF]).astype(bf16)

    near_t[...] = jnp.zeros((LEAF_DEV, LEAF, 2 * RHS), f32)

    def one_block(entry):
        leaf = work[0, entry]
        source = work[1, entry]
        uses = work[2, entry].astype(f32)
        both = bf16_dot(targets[leaf], sources[source])
        inverse = lax.rsqrt(both[:, :LEAF])
        block = both[:, LEAF:] * (inverse * inverse * inverse)
        high, low = two_parts(block)
        term = lax.dot_general(
            jnp.concatenate([high, low], axis=1),
            dens_parts[source],
            (((1,), (1,)), ((), ())),
            preferred_element_type=f32,
        )
        return leaf, uses * term

    def blocks_from(first, size):
        results = [one_block(first + k) for k in range(size)]
        for leaf, term in results:
            near_t[leaf] = near_t[leaf] + term

    def many_blocks(step, carry):
        blocks_from(2 * GROUP * step, 2 * GROUP)
        return carry

    def some_blocks(step, carry):
        blocks_from(GROUP * step, GROUP)
        return carry

    groups = (count + GROUP - 1) // GROUP
    lax.fori_loop(0, groups // 2, many_blocks, 0)
    lax.fori_loop(groups // 2 * 2, groups, some_blocks, 0)
    for leaf in range(LEAF_DEV):
        total = jnp.transpose(near_t[leaf])
        near_out[leaf] = 0.5 * own[0:RHS, LEAF * leaf : LEAF * leaf + LEAF] + total[:RHS] + total[RHS:]

    for side in range(3):
        for c in range(LEAF_DEV):
            split_leaf[LEAF_DEV * side + c] = unpack(halo[side][COEF_ROW:, 128 * c : 128 * c + 128])
        for m in range(MID_DEV):
            lanes = slice(128 * (LEAF_DEV + m), 128 * (LEAF_DEV + m) + 128)
            split_mid[MID_DEV * side + m] = unpack(halo[side][COEF_ROW:, lanes])
    for couple, number, adm, split, offset, result in (
        (couple_leaf, LEAF_DEV, adm_leaf, split_leaf, first_leaf, leaf_couple),
        (couple_mid, MID_DEV, adm_mid, split_mid, first_mid, mid_couple),
    ):
        slots = couple.shape[0]
        for a in range(slots):
            for chunk in range(CHUNKS):
                rows[a, 8 * chunk : 8 * chunk + number, :] = couple[a, :, 128 * chunk : 128 * chunk + 128]
        for t in range(number):
            lhs = jnp.concatenate([rows[a, pl.ds(t, CHUNKS, stride=8), :] for a in range(slots)], axis=0)
            rhs = jnp.concatenate([split[held(adm[t, a] - offset + number, number)] for a in range(slots)], axis=0)
            result[t] = fold(dot(lhs, rhs, 0, 0))
    for c in range(LEAF_DEV):
        cols = slice(LEAF * c, LEAF * c + LEAF)
        field = leaf_couple[c] + dot(leaf_mats[c], mid_couple[c // 2])
        base[:, cols] = near_out[c] + dot(field, row_basis[:, cols], 0, 0)


def matrix_kernel(couple_top, down_mid, down_leaf, row_basis, top_mats, leaf_mats, top_to_points, mid_mats, rows, natural):
    for chunk in range(CHUNKS):
        rows[16 * chunk : 16 * chunk + ADM_TOP, :] = couple_top[0, :, 128 * chunk : 128 * chunk + 128]
    for group in range(4):
        stack = jnp.concatenate(
            [rows[pl.ds(4 * group + a, CHUNKS, stride=16), :] for a in range(4)], axis=0
        )
        high, low = two_parts(jnp.transpose(stack))
        top_mats[0:128, 128 * group : 128 * group + 128] = high
        top_mats[128:, 128 * group : 128 * group + 128] = low
    for source, result, number in ((down_mid, mid_mats, MID_DEV), (down_leaf, leaf_mats, LEAF_DEV)):
        for chunk in range(CHUNKS):
            rows[8 * chunk : 8 * chunk + number, :] = source[:, 128 * chunk : 128 * chunk + 128]
        for c in range(number):
            wide = rows[pl.ds(c, CHUNKS, stride=8), :]
            swapped = jnp.concatenate([wide[:, RANK:], wide[:, :RANK]], axis=1)
            natural[pl.ds(0, HALF, stride=2), :] = wide
            natural[pl.ds(1, HALF, stride=2), :] = swapped
            result[c] = jnp.transpose(natural[...])[:RANK]
    for c in range(LEAF_DEV):
        cols = slice(LEAF * c, LEAF * c + LEAF)
        high, low = two_parts(dot(dot(leaf_mats[c], mid_mats[c // 2]), row_basis[:, cols], 0, 0))
        top_to_points[0:RANK, cols] = high
        top_to_points[RANK : 2 * RANK, cols] = high
        top_to_points[2 * RANK :, cols] = low


def matrix_call(*operands):
    return pl.pallas_call(
        matrix_kernel,
        name="transposed_matrices",
        out_shape=(
            jax.ShapeDtypeStruct((256, ADM_TOP * HALF), bf16),
            jax.ShapeDtypeStruct((LEAF_DEV, RANK, RANK), f32),
            jax.ShapeDtypeStruct((3 * RANK, SPAN), bf16),
        ),
        in_specs=[VMEM] * 4,
        out_specs=(VMEM,) * 3,
        scratch_shapes=[
            pltpu.VMEM((MID_DEV, RANK, RANK), f32),
            pltpu.VMEM((16 * CHUNKS, 128), f32),
            pltpu.VMEM((RANK, 128), f32),
        ],
        compiler_params=pltpu.CompilerParams(vmem_limit_bytes=VMEM_LIMIT),
        cost_estimate=pl.CostEstimate(flops=2_000_000_000, bytes_accessed=2_000_000, transcendentals=0),
    )(*operands)


def near_call(near_list, near_count, adm_leaf, adm_mid, *rest):
    return pl.pallas_call(
        near_kernel,
        name="near_and_couplings",
        out_shape=(
            jax.ShapeDtypeStruct((RHS, SPAN), f32),
            jax.ShapeDtypeStruct((4, ADM_TOP), jnp.int32),
        ),
        in_specs=[SMEM] * 4 + [VMEM] * 7 + [SMEM] * 2,
        out_specs=(VMEM, SMEM),
        scratch_shapes=[
            pltpu.VMEM((LEAF_DEV, RHS, LEAF), f32),
            pltpu.VMEM((LEAF_DEV, LEAF, 2 * RHS), f32),
            pltpu.VMEM((LEAF_DEV, RANK, RHS), f32),
            pltpu.VMEM((MID_DEV, RANK, RHS), f32),
            pltpu.VMEM((2 * FEATURES, SPAN), f32),
            pltpu.VMEM((3 * LEAF_DEV, FEATURES, 2 * LEAF), bf16),
            pltpu.VMEM((LEAF_DEV, LEAF, FEATURES), bf16),
            pltpu.VMEM((3 * LEAF_DEV, 2 * RHS, 2 * LEAF), bf16),
            pltpu.VMEM((3 * LEAF_DEV, HALF, HALF), f32),
            pltpu.VMEM((3 * MID_DEV, HALF, HALF), f32),
            pltpu.VMEM((ADM_LEAF, 8 * CHUNKS, 128), f32),
            pltpu.SMEM((3, LEAF_DEV * NEAR + 8), jnp.int32),
        ],
        compiler_params=pltpu.CompilerParams(vmem_limit_bytes=VMEM_LIMIT),
        cost_estimate=pl.CostEstimate(flops=4_000_000_000, bytes_accessed=2_000_000, transcendentals=2_000_000),
    )(near_list, near_count, adm_leaf, adm_mid, *rest)


def top_share(top_mats, chosen):
    high, low = two_parts(chosen)
    product = bf16_dot(top_mats[...], jnp.concatenate([high, low], axis=1))
    width = 2 * RHS
    return fold(product[:128, :width] + product[:128, width:] + product[128:, :width])


def held_tops(plan, row, tops):
    return [
        jnp.where(plan[row + 1, a] == 1, tops[plan[row, a]], jnp.zeros((8, 128), f32)) for a in range(ADM_TOP)
    ]


def answer_kernel(plan, own_tops, out):
    for a, tile in enumerate(held_tops(plan, 2, own_tops)):
        out[a] = tile


def answer_call(plan, own_tops):
    return pl.pallas_call(
        answer_kernel,
        name="answer",
        out_shape=jax.ShapeDtypeStruct((ADM_TOP, 8, 128), f32),
        in_specs=[SMEM, VMEM],
        out_specs=VMEM,
        compiler_params=pltpu.CompilerParams(vmem_limit_bytes=VMEM_LIMIT),
        cost_estimate=pl.CostEstimate(flops=1_000_000, bytes_accessed=100_000, transcendentals=0),
    )(plan, own_tops)


def own_kernel(plan, own_tops, top_mats, out):
    out[...] = top_share(top_mats, jnp.concatenate([unpack(tile) for tile in held_tops(plan, 0, own_tops)], axis=0))


def own_call(plan, own_tops, top_mats):
    return pl.pallas_call(
        own_kernel,
        name="own_tops",
        out_shape=jax.ShapeDtypeStruct((RANK, RHS), f32),
        in_specs=[SMEM, VMEM, VMEM],
        out_specs=VMEM,
        compiler_params=pltpu.CompilerParams(vmem_limit_bytes=VMEM_LIMIT),
        cost_estimate=pl.CostEstimate(flops=400_000_000, bytes_accessed=400_000, transcendentals=0),
    )(plan, own_tops, top_mats)


def down_kernel(received, own_share, base, top_mats, top_to_points, out):
    chosen = jnp.concatenate([unpack(received[a]) for a in range(ADM_TOP)], axis=0)
    top_field = own_share[...] + top_share(top_mats, chosen)
    high, low = two_parts(jnp.transpose(top_field))
    out[...] = base[...] + bf16_dot(jnp.concatenate([high, low, high], axis=1), top_to_points[...])


def down_call(*operands):
    return pl.pallas_call(
        down_kernel,
        name="down_sweep",
        out_shape=jax.ShapeDtypeStruct((RHS, SPAN), f32),
        in_specs=[VMEM] * 5,
        out_specs=VMEM,
        compiler_params=pltpu.CompilerParams(vmem_limit_bytes=VMEM_LIMIT),
        cost_estimate=pl.CostEstimate(flops=10_000_000, bytes_accessed=800_000, transcendentals=0),
    )(*operands)


def solution(mesh):
    devices = mesh.devices.size
    ring = [(FIRST_Z + i) % RING for i in range(RING)]
    planes = [(FIRST_PLANE + i) % PLANES for i in range(PLANES)]
    along_z = [[(p * RING + z) * CORES + c for z in ring] for p in range(PLANES) for c in range(CORES)]
    across = [[(p * RING + z) * CORES + c for p in planes] for z in range(RING) for c in range(CORES)]

    def on_device(
        densities,
        points,
        area_normals,
        col_basis,
        row_basis,
        up_leaf,
        up_mid,
        down_leaf,
        down_mid,
        couple_leaf,
        couple_mid,
        couple_top,
        near_list,
        near_count,
        adm_leaf,
        adm_mid,
        adm_top,
    ):
        own_top, coefs = up_call(densities, col_basis, up_leaf, up_mid, RING)
        own_top, coefs, couple_top, down_mid, down_leaf = lax.optimization_barrier(
            (own_top, coefs, couple_top, down_mid, down_leaf)
        )
        packed = pack_call(densities, points, area_normals, coefs, adm_top)
        ring_tops = lax.all_to_all(own_top, "leaf", 0, 0, axis_index_groups=along_z, tiled=True)
        same_chip = lax.ppermute(packed, "leaf", [(i, i ^ 1) for i in range(devices)])
        next_chip = lax.ppermute(packed, "leaf", [(i, ((i + 1) ^ 1) - 1) for i in range(1, devices - 1)])
        top_mats, leaf_mats, top_to_points = matrix_call(couple_top, down_mid, down_leaf, row_basis)
        ring_tops, same_chip, next_chip, top_mats, leaf_mats, top_to_points = lax.optimization_barrier(
            (ring_tops, same_chip, next_chip, top_mats, leaf_mats, top_to_points)
        )
        spread = jnp.broadcast_to(ring_tops.reshape(1, RING * 8, 128), (PLANES, RING * 8, 128))
        core_tops = lax.all_to_all(spread, "leaf", 0, 0, axis_index_groups=across, tiled=True)
        wanted = same_chip[WANTED_ROW : WANTED_ROW + 1, 0:ADM_TOP].astype(jnp.int32)
        base, plan = near_call(
            near_list,
            near_count,
            adm_leaf,
            adm_mid,
            packed,
            same_chip,
            next_chip,
            jnp.swapaxes(couple_leaf, 0, 1),
            jnp.swapaxes(couple_mid, 0, 1),
            leaf_mats,
            row_basis,
            adm_top,
            wanted,
        )
        core_tops, base, plan = lax.optimization_barrier((core_tops, base, plan))
        core_tops = core_tops.reshape(PLANES * RING, 8, 128)
        answers = answer_call(plan, core_tops)
        received = lax.ppermute(answers, "leaf", [(i, i ^ 1) for i in range(devices)])
        answers, plan, core_tops = lax.optimization_barrier((answers, plan, core_tops))
        own_share = own_call(plan, core_tops, top_mats)
        return down_call(
            received,
            own_share,
            base,
            top_mats,
            top_to_points,
        )

    split_last = P(None, "leaf")
    split_first = P("leaf", None)
    split_three = P("leaf", None, None)
    return jax.shard_map(
        on_device,
        mesh=mesh,
        in_specs=(split_last,) * 5
        + (split_first,) * 4
        + (split_three,) * 3
        + (split_first, P("leaf"), split_first, split_first, split_first),
        out_specs=split_last,
        check_vma=False,
    )
```

```python
import math

import jax
import jax.numpy as jnp
from jax import lax
from jax.experimental import pallas as pl
from jax.experimental.pallas import tpu as pltpu
from jax.sharding import PartitionSpec as P

RHS = 16
LEAF = 256
RANK = 64
HALF = RANK // 2
LEAF_DEV = 4
MID_DEV = 2
NEAR = 8
ADM_LEAF = 6
ADM_MID = 6
ADM_TOP = 16
SPAN = LEAF_DEV * LEAF
CHUNKS = RANK * RANK // 128
FEATURES = 32
PACKED_ROWS = 32
WANTED_ROW = 22
COEF_ROW = 24
GROUP = 8
VMEM_LIMIT = 16 * 1024 * 1024
CORES = 2
RING = 16
PLANES = 16
FIRST_Z = 12
FIRST_PLANE = 10

smooth_sq = 0.01
four_pi = 4.0 * math.pi
highest = lax.Precision.HIGHEST
f32 = jnp.float32
bf16 = jnp.bfloat16

SMEM = pl.BlockSpec(memory_space=pltpu.SMEM)
VMEM = pl.BlockSpec(memory_space=pltpu.VMEM)


def dot(lhs, rhs, lhs_dim=1, rhs_dim=0):
    return lax.dot_general(
        lhs,
        rhs,
        (((lhs_dim,), (rhs_dim,)), ((), ())),
        precision=highest,
        preferred_element_type=f32,
    )


def even_odd(ref, index):
    even = ref[index, pl.ds(0, HALF, stride=2), :]
    odd = ref[index, pl.ds(1, HALF, stride=2), :]
    return jnp.concatenate([even[:, :RHS], odd[:, :RHS]], axis=1)


def pack(split):
    return jnp.concatenate([split[8 * g : 8 * g + 8] for g in range(4)], axis=1)


def unpack(tile):
    return jnp.concatenate([tile[:, 32 * g : 32 * g + 32] for g in range(4)], axis=0)


def fold(product):
    return product[:RANK, :RHS] + product[RANK:, RHS:]


def dot_parts(lhs, rhs, lhs_dim=1, rhs_dim=0):
    lhs_high, lhs_low = two_parts(lhs)
    rhs_high, rhs_low = two_parts(rhs)
    return lax.dot_general(
        jnp.concatenate([lhs_high, lhs_high, lhs_low], axis=lhs_dim),
        jnp.concatenate([rhs_high, rhs_low, rhs_high], axis=rhs_dim),
        (((lhs_dim,), (rhs_dim,)), ((), ())),
        preferred_element_type=f32,
    )


def up_kernel(dens, col_basis, up_leaf, up_mid, top_out, coefs, leaf_rows, mid_rows, leaf_t, mid_t):
    for chunk in range(CHUNKS):
        lanes = slice(128 * chunk, 128 * chunk + 128)
        leaf_rows[8 * chunk : 8 * chunk + LEAF_DEV, :] = up_leaf[:, lanes]
        mid_rows[8 * chunk : 8 * chunk + MID_DEV, :] = up_mid[:, lanes]
    for c in range(LEAF_DEV):
        cols = slice(LEAF * c, LEAF * c + LEAF)
        leaf_t[c, :, 0:RHS] = dot_parts(col_basis[:, cols], dens[:, cols], 1, 1)
    leaf_split = [even_odd(leaf_t, c) for c in range(LEAF_DEV)]
    for c in range(LEAF_DEV):
        coefs[:, 128 * c : 128 * c + 128] = pack(leaf_split[c])
    for m in range(MID_DEV):
        pair = (2 * m, 2 * m + 1)
        lhs = jnp.concatenate([leaf_rows[pl.ds(c, CHUNKS, stride=8), :] for c in pair], axis=0)
        rhs = jnp.concatenate([leaf_split[c] for c in pair], axis=0)
        mid_t[m, :, 0:RHS] = fold(dot_parts(lhs, rhs, 0, 0))
    mid_split = [even_odd(mid_t, m) for m in range(MID_DEV)]
    for m in range(MID_DEV):
        coefs[:, 128 * (LEAF_DEV + m) : 128 * (LEAF_DEV + m) + 128] = pack(mid_split[m])
    lhs = jnp.concatenate([mid_rows[pl.ds(m, CHUNKS, stride=8), :] for m in range(MID_DEV)], axis=0)
    rhs = jnp.concatenate(mid_split, axis=0)
    leaf_t[0, :, 0:RHS] = fold(dot_parts(lhs, rhs, 0, 0))
    tile = pack(even_odd(leaf_t, 0))
    for peer in range(top_out.shape[0]):
        top_out[peer] = tile


def pack_kernel(dens, points, normals, coefs, adm_top, packed):
    packed[0:RHS, :] = dens[...]
    packed[RHS : RHS + 3, :] = points[...]
    packed[RHS + 3 : RHS + 6, :] = normals[...]
    packed[WANTED_ROW:COEF_ROW, :] = jnp.zeros((COEF_ROW - WANTED_ROW, SPAN), f32)
    packed[WANTED_ROW : WANTED_ROW + 1, 0:ADM_TOP] = adm_top[...].astype(f32)
    packed[COEF_ROW:, 0 : 6 * 128] = coefs[...]
    packed[COEF_ROW:, 6 * 128 :] = jnp.zeros((8, SPAN - 6 * 128), f32)


def pack_call(*operands):
    return pl.pallas_call(
        pack_kernel,
        name="packed_for_neighbours",
        out_shape=jax.ShapeDtypeStruct((PACKED_ROWS, SPAN), f32),
        in_specs=[VMEM] * 5,
        out_specs=VMEM,
        compiler_params=pltpu.CompilerParams(vmem_limit_bytes=VMEM_LIMIT),
        cost_estimate=pl.CostEstimate(flops=100_000_000, bytes_accessed=400_000, transcendentals=0),
    )(*operands)


def up_call(dens, col_basis, up_leaf, up_mid, peers):
    return pl.pallas_call(
        up_kernel,
        name="up_sweep",
        out_shape=(
            jax.ShapeDtypeStruct((peers, 8, 128), f32),
            jax.ShapeDtypeStruct((8, 6 * 128), f32),
        ),
        in_specs=[VMEM] * 4,
        out_specs=(VMEM, VMEM),
        scratch_shapes=[
            pltpu.VMEM((8 * CHUNKS, 128), f32),
            pltpu.VMEM((8 * CHUNKS, 128), f32),
            pltpu.VMEM((LEAF_DEV, RANK, 128), f32),
            pltpu.VMEM((MID_DEV, RANK, 128), f32),
        ],
        cost_estimate=pl.CostEstimate(flops=10_000_000, bytes_accessed=800_000, transcendentals=0),
    )(dens, col_basis, up_leaf, up_mid)


def two_parts(values):
    first = values.astype(bf16)
    return first, (values - first.astype(f32)).astype(bf16)


def bf16_dot(lhs, rhs):
    return lax.dot_general(lhs, rhs, (((1,), (0,)), ((), ())), preferred_element_type=f32)


def three_parts(values):
    first = values.astype(bf16).astype(f32)
    rest = values - first
    second = rest.astype(bf16).astype(f32)
    return first, second, (rest - second).astype(bf16).astype(f32)


def near_kernel(
    near_list,
    near_count,
    adm_leaf,
    adm_mid,
    own,
    same_chip,
    next_chip,
    couple_leaf,
    couple_mid,
    leaf_mats,
    row_basis,
    adm_top,
    wanted,
    base,
    plan,
    near_out,
    near_t,
    leaf_couple,
    mid_couple,
    feats,
    sources,
    targets,
    dens_parts,
    split_leaf,
    split_mid,
    rows,
    work,
):
    halo = (same_chip, own, next_chip)
    first_leaf = near_list[0, 0]
    first_mid = first_leaf // 2
    core = (first_leaf // LEAF_DEV) % 2

    def held(place, number):
        side = place // number
        return jnp.where(core == 0, place + (2 - 2 * side) * number, place)

    for row, tops in ((0, adm_top), (2, wanted)):
        for a in range(ADM_TOP):
            plane = tops[0, a] // (CORES * RING)
            z = tops[0, a] // CORES % RING
            plan[row, a] = (plane + PLANES - FIRST_PLANE) % PLANES * RING + (z + RING - FIRST_Z) % RING
            plan[row + 1, a] = (tops[0, a] % CORES == core).astype(jnp.int32)

    count = jnp.int32(0)
    for i in range(LEAF_DEV):
        limit = near_count[i]
        slots = [near_list[i, j] for j in range(NEAR)]
        used = [jnp.int32(j) < limit for j in range(NEAR)]
        for j in range(NEAR):
            uses = jnp.int32(0)
            fresh = used[j]
            for other in range(NEAR):
                same = jnp.logical_and(used[other], slots[other] == slots[j])
                uses = uses + same.astype(jnp.int32)
                if other < j:
                    fresh = jnp.logical_and(fresh, jnp.logical_not(same))
            work[0, count] = jnp.int32(i)
            work[1, count] = held(slots[j] - first_leaf + LEAF_DEV, LEAF_DEV)
            work[2, count] = uses
            count = count + fresh.astype(jnp.int32)
    for extra in range(GROUP):
        work[0, count + extra] = jnp.int32(0)
        work[1, count + extra] = jnp.int32(0)
        work[2, count + extra] = jnp.int32(0)

    for side in range(3):
        block = halo[side]
        place = block[RHS : RHS + 3, :] - 0.5
        normal = block[RHS + 3 : RHS + 6, :] * (1.0 / four_pi)
        p1, p2, p3 = three_parts(place)
        n1, n2, n3 = three_parts(normal)
        square = jnp.sum(place * place, axis=0, keepdims=True)
        inner = -jnp.sum(place * normal, axis=0, keepdims=True)
        ones = jnp.ones((3, SPAN), f32)
        zeros = jnp.zeros((8, SPAN), f32)
        s1, s2, s3 = three_parts(square)
        i1, i2, i3 = three_parts(inner)
        feats[0:1], feats[1:2], feats[2:3] = s1, s2, s3
        feats[3:6] = ones
        for slot, part in enumerate((p1, p1, p2, p2, p1, p3)):
            feats[6 + 3 * slot : 9 + 3 * slot] = part * -2.0
        feats[24:32] = zeros
        feats[32:40] = zeros
        feats[32:33], feats[33:34], feats[34:35] = i1, i2, i3
        for slot, part in enumerate((n1, n1, n2, n2, n1, n3)):
            feats[38 + 3 * slot : 41 + 3 * slot] = part
        feats[56:64] = zeros
        for leaf in range(LEAF_DEV):
            cols = slice(LEAF * leaf, LEAF * leaf + LEAF)
            place_held = LEAF_DEV * side + leaf
            sources[place_held, :, 0:LEAF] = feats[0:FEATURES, cols].astype(bf16)
            sources[place_held, :, LEAF:] = feats[FEATURES:, cols].astype(bf16)
            dens_high, dens_low = two_parts(block[0:RHS, cols])
            dens_parts[place_held, 0:RHS, 0:LEAF] = dens_high
            dens_parts[place_held, 0:RHS, LEAF:] = dens_high
            dens_parts[place_held, RHS:, 0:LEAF] = dens_low
            dens_parts[place_held, RHS:, LEAF:] = jnp.zeros((RHS, LEAF), bf16)
        if side == 1:
            t1, t2, t3 = three_parts(square + smooth_sq)
            feats[0:3] = ones
            feats[3:4], feats[4:5], feats[5:6] = t1, t2, t3
            for slot, part in enumerate((p1, p2, p1, p2, p3, p1)):
                feats[6 + 3 * slot : 9 + 3 * slot] = part
            feats[24:32] = zeros
            for leaf in range(LEAF_DEV):
                targets[leaf] = jnp.transpose(feats[0:FEATURES, LEAF * leaf : LEAF * leaf + LEAF]).astype(bf16)

    near_t[...] = jnp.zeros((LEAF_DEV, LEAF, 2 * RHS), f32)

    def one_block(entry):
        leaf = work[0, entry]
        source = work[1, entry]
        uses = work[2, entry].astype(f32)
        both = bf16_dot(targets[leaf], sources[source])
        inverse = lax.rsqrt(both[:, :LEAF])
        block = both[:, LEAF:] * (inverse * inverse * inverse)
        high, low = two_parts(block)
        term = lax.dot_general(
            jnp.concatenate([high, low], axis=1),
            dens_parts[source],
            (((1,), (1,)), ((), ())),
            preferred_element_type=f32,
        )
        return leaf, uses * term

    def blocks_from(first, size):
        results = [one_block(first + k) for k in range(size)]
        for leaf, term in results:
            near_t[leaf] = near_t[leaf] + term

    def many_blocks(step, carry):
        blocks_from(2 * GROUP * step, 2 * GROUP)
        return carry

    def some_blocks(step, carry):
        blocks_from(GROUP * step, GROUP)
        return carry

    groups = (count + GROUP - 1) // GROUP
    lax.fori_loop(0, groups // 2, many_blocks, 0)
    lax.fori_loop(groups // 2 * 2, groups, some_blocks, 0)
    for leaf in range(LEAF_DEV):
        total = jnp.transpose(near_t[leaf])
        near_out[leaf] = 0.5 * own[0:RHS, LEAF * leaf : LEAF * leaf + LEAF] + total[:RHS] + total[RHS:]

    for side in range(3):
        for c in range(LEAF_DEV):
            split_leaf[LEAF_DEV * side + c] = unpack(halo[side][COEF_ROW:, 128 * c : 128 * c + 128])
        for m in range(MID_DEV):
            lanes = slice(128 * (LEAF_DEV + m), 128 * (LEAF_DEV + m) + 128)
            split_mid[MID_DEV * side + m] = unpack(halo[side][COEF_ROW:, lanes])
    for couple, number, adm, split, offset, result in (
        (couple_leaf, LEAF_DEV, adm_leaf, split_leaf, first_leaf, leaf_couple),
        (couple_mid, MID_DEV, adm_mid, split_mid, first_mid, mid_couple),
    ):
        slots = couple.shape[0]
        for a in range(slots):
            for chunk in range(CHUNKS):
                rows[a, 8 * chunk : 8 * chunk + number, :] = couple[a, :, 128 * chunk : 128 * chunk + 128]
        for t in range(number):
            lhs = jnp.concatenate([rows[a, pl.ds(t, CHUNKS, stride=8), :] for a in range(slots)], axis=0)
            rhs = jnp.concatenate([split[held(adm[t, a] - offset + number, number)] for a in range(slots)], axis=0)
            result[t] = fold(dot(lhs, rhs, 0, 0))
    for c in range(LEAF_DEV):
        cols = slice(LEAF * c, LEAF * c + LEAF)
        field = leaf_couple[c] + dot(leaf_mats[c], mid_couple[c // 2])
        base[:, cols] = near_out[c] + dot(field, row_basis[:, cols], 0, 0)


def matrix_kernel(couple_top, down_mid, down_leaf, row_basis, top_mats, leaf_mats, top_to_points, mid_mats, rows, natural):
    for chunk in range(CHUNKS):
        rows[16 * chunk : 16 * chunk + ADM_TOP, :] = couple_top[0, :, 128 * chunk : 128 * chunk + 128]
    for group in range(4):
        stack = jnp.concatenate(
            [rows[pl.ds(4 * group + a, CHUNKS, stride=16), :] for a in range(4)], axis=0
        )
        high, low = two_parts(jnp.transpose(stack))
        top_mats[0:128, 128 * group : 128 * group + 128] = high
        top_mats[128:, 128 * group : 128 * group + 128] = low
    for source, result, number in ((down_mid, mid_mats, MID_DEV), (down_leaf, leaf_mats, LEAF_DEV)):
        for chunk in range(CHUNKS):
            rows[8 * chunk : 8 * chunk + number, :] = source[:, 128 * chunk : 128 * chunk + 128]
        for c in range(number):
            wide = rows[pl.ds(c, CHUNKS, stride=8), :]
            swapped = jnp.concatenate([wide[:, RANK:], wide[:, :RANK]], axis=1)
            natural[pl.ds(0, HALF, stride=2), :] = wide
            natural[pl.ds(1, HALF, stride=2), :] = swapped
            result[c] = jnp.transpose(natural[...])[:RANK]
    for c in range(LEAF_DEV):
        cols = slice(LEAF * c, LEAF * c + LEAF)
        high, low = two_parts(dot(dot(leaf_mats[c], mid_mats[c // 2]), row_basis[:, cols], 0, 0))
        top_to_points[0:RANK, cols] = high
        top_to_points[RANK : 2 * RANK, cols] = high
        top_to_points[2 * RANK :, cols] = low


def matrix_call(*operands):
    return pl.pallas_call(
        matrix_kernel,
        name="transposed_matrices",
        out_shape=(
            jax.ShapeDtypeStruct((256, ADM_TOP * HALF), bf16),
            jax.ShapeDtypeStruct((LEAF_DEV, RANK, RANK), f32),
            jax.ShapeDtypeStruct((3 * RANK, SPAN), bf16),
        ),
        in_specs=[VMEM] * 4,
        out_specs=(VMEM,) * 3,
        scratch_shapes=[
            pltpu.VMEM((MID_DEV, RANK, RANK), f32),
            pltpu.VMEM((16 * CHUNKS, 128), f32),
            pltpu.VMEM((RANK, 128), f32),
        ],
        compiler_params=pltpu.CompilerParams(vmem_limit_bytes=VMEM_LIMIT),
        cost_estimate=pl.CostEstimate(flops=2_000_000_000, bytes_accessed=2_000_000, transcendentals=0),
    )(*operands)


def near_call(near_list, near_count, adm_leaf, adm_mid, *rest):
    return pl.pallas_call(
        near_kernel,
        name="near_and_couplings",
        out_shape=(
            jax.ShapeDtypeStruct((RHS, SPAN), f32),
            jax.ShapeDtypeStruct((4, ADM_TOP), jnp.int32),
        ),
        in_specs=[SMEM] * 4 + [VMEM] * 7 + [SMEM] * 2,
        out_specs=(VMEM, SMEM),
        scratch_shapes=[
            pltpu.VMEM((LEAF_DEV, RHS, LEAF), f32),
            pltpu.VMEM((LEAF_DEV, LEAF, 2 * RHS), f32),
            pltpu.VMEM((LEAF_DEV, RANK, RHS), f32),
            pltpu.VMEM((MID_DEV, RANK, RHS), f32),
            pltpu.VMEM((2 * FEATURES, SPAN), f32),
            pltpu.VMEM((3 * LEAF_DEV, FEATURES, 2 * LEAF), bf16),
            pltpu.VMEM((LEAF_DEV, LEAF, FEATURES), bf16),
            pltpu.VMEM((3 * LEAF_DEV, 2 * RHS, 2 * LEAF), bf16),
            pltpu.VMEM((3 * LEAF_DEV, HALF, HALF), f32),
            pltpu.VMEM((3 * MID_DEV, HALF, HALF), f32),
            pltpu.VMEM((ADM_LEAF, 8 * CHUNKS, 128), f32),
            pltpu.SMEM((3, LEAF_DEV * NEAR + 8), jnp.int32),
        ],
        compiler_params=pltpu.CompilerParams(vmem_limit_bytes=VMEM_LIMIT),
        cost_estimate=pl.CostEstimate(flops=4_000_000_000, bytes_accessed=2_000_000, transcendentals=2_000_000),
    )(near_list, near_count, adm_leaf, adm_mid, *rest)


def top_share(top_mats, chosen):
    high, low = two_parts(chosen)
    product = bf16_dot(top_mats[...], jnp.concatenate([high, low], axis=1))
    width = 2 * RHS
    return fold(product[:128, :width] + product[:128, width:] + product[128:, :width])


def held_tops(plan, row, tops):
    return [
        jnp.where(plan[row + 1, a] == 1, tops[plan[row, a]], jnp.zeros((8, 128), f32)) for a in range(ADM_TOP)
    ]


def answer_kernel(plan, own_tops, out):
    for a, tile in enumerate(held_tops(plan, 2, own_tops)):
        out[a] = tile


def answer_call(plan, own_tops):
    return pl.pallas_call(
        answer_kernel,
        name="answer",
        out_shape=jax.ShapeDtypeStruct((ADM_TOP, 8, 128), f32),
        in_specs=[SMEM, VMEM],
        out_specs=VMEM,
        compiler_params=pltpu.CompilerParams(vmem_limit_bytes=VMEM_LIMIT),
        cost_estimate=pl.CostEstimate(flops=1_000_000, bytes_accessed=100_000, transcendentals=0),
    )(plan, own_tops)


def own_kernel(plan, own_tops, top_mats, out):
    out[...] = top_share(top_mats, jnp.concatenate([unpack(tile) for tile in held_tops(plan, 0, own_tops)], axis=0))


def own_call(plan, own_tops, top_mats):
    return pl.pallas_call(
        own_kernel,
        name="own_tops",
        out_shape=jax.ShapeDtypeStruct((RANK, RHS), f32),
        in_specs=[SMEM, VMEM, VMEM],
        out_specs=VMEM,
        compiler_params=pltpu.CompilerParams(vmem_limit_bytes=VMEM_LIMIT),
        cost_estimate=pl.CostEstimate(flops=400_000_000, bytes_accessed=400_000, transcendentals=0),
    )(plan, own_tops, top_mats)


def down_kernel(received, own_share, base, top_mats, top_to_points, out):
    chosen = jnp.concatenate([unpack(received[a]) for a in range(ADM_TOP)], axis=0)
    top_field = own_share[...] + top_share(top_mats, chosen)
    high, low = two_parts(jnp.transpose(top_field))
    out[...] = base[...] + bf16_dot(jnp.concatenate([high, low, high], axis=1), top_to_points[...])


def down_call(*operands):
    return pl.pallas_call(
        down_kernel,
        name="down_sweep",
        out_shape=jax.ShapeDtypeStruct((RHS, SPAN), f32),
        in_specs=[VMEM] * 5,
        out_specs=VMEM,
        compiler_params=pltpu.CompilerParams(vmem_limit_bytes=VMEM_LIMIT),
        cost_estimate=pl.CostEstimate(flops=10_000_000, bytes_accessed=800_000, transcendentals=0),
    )(*operands)


def solution(mesh):
    devices = mesh.devices.size
    ring = [(FIRST_Z + i) % RING for i in range(RING)]
    planes = [(FIRST_PLANE + i) % PLANES for i in range(PLANES)]
    along_z = [[(p * RING + z) * CORES + c for z in ring] for p in range(PLANES) for c in range(CORES)]
    across = [[(p * RING + z) * CORES + c for p in planes] for z in range(RING) for c in range(CORES)]

    def on_device(
        densities,
        points,
        area_normals,
        col_basis,
        row_basis,
        up_leaf,
        up_mid,
        down_leaf,
        down_mid,
        couple_leaf,
        couple_mid,
        couple_top,
        near_list,
        near_count,
        adm_leaf,
        adm_mid,
        adm_top,
    ):
        own_top, coefs = up_call(densities, col_basis, up_leaf, up_mid, RING)
        own_top, coefs, couple_top, down_mid, down_leaf = lax.optimization_barrier(
            (own_top, coefs, couple_top, down_mid, down_leaf)
        )
        packed = pack_call(densities, points, area_normals, coefs, adm_top)
        ring_tops = lax.all_to_all(own_top, "leaf", 0, 0, axis_index_groups=along_z, tiled=True)
        same_chip = lax.ppermute(packed, "leaf", [(i, i ^ 1) for i in range(devices)])
        next_chip = lax.ppermute(packed, "leaf", [(i, ((i + 1) ^ 1) - 1) for i in range(1, devices - 1)])
        top_mats, leaf_mats, top_to_points = matrix_call(couple_top, down_mid, down_leaf, row_basis)
        ring_tops, same_chip, next_chip, top_mats, leaf_mats, top_to_points = lax.optimization_barrier(
            (ring_tops, same_chip, next_chip, top_mats, leaf_mats, top_to_points)
        )
        spread = jnp.broadcast_to(ring_tops.reshape(1, RING * 8, 128), (PLANES, RING * 8, 128))
        core_tops = lax.all_to_all(spread, "leaf", 0, 0, axis_index_groups=across, tiled=True)
        wanted = same_chip[WANTED_ROW : WANTED_ROW + 1, 0:ADM_TOP].astype(jnp.int32)
        base, plan = near_call(
            near_list,
            near_count,
            adm_leaf,
            adm_mid,
            packed,
            same_chip,
            next_chip,
            jnp.swapaxes(couple_leaf, 0, 1),
            jnp.swapaxes(couple_mid, 0, 1),
            leaf_mats,
            row_basis,
            adm_top,
            wanted,
        )
        core_tops, base, plan = lax.optimization_barrier((core_tops, base, plan))
        core_tops = core_tops.reshape(PLANES * RING, 8, 128)
        answers = answer_call(plan, core_tops)
        received = lax.ppermute(answers, "leaf", [(i, i ^ 1) for i in range(devices)])
        answers, plan, core_tops = lax.optimization_barrier((answers, plan, core_tops))
        own_share = own_call(plan, core_tops, top_mats)
        return down_call(
            received,
            own_share,
            base,
            top_mats,
            top_to_points,
        )

    split_last = P(None, "leaf")
    split_first = P("leaf", None)
    split_three = P("leaf", None, None)
    return jax.shard_map(
        on_device,
        mesh=mesh,
        in_specs=(split_last,) * 5
        + (split_first,) * 4
        + (split_three,) * 3
        + (split_first, P("leaf"), split_first, split_first, split_first),
        out_specs=split_last,
        check_vma=False,
    )
```

```python
import math

import jax
import jax.numpy as jnp
from jax import lax
from jax.experimental import pallas as pl
from jax.experimental.pallas import tpu as pltpu
from jax.sharding import PartitionSpec as P

RHS = 16
LEAF = 256
RANK = 64
HALF = RANK // 2
LEAF_DEV = 4
MID_DEV = 2
NEAR = 8
ADM_LEAF = 6
ADM_MID = 6
ADM_TOP = 16
SPAN = LEAF_DEV * LEAF
CHUNKS = RANK * RANK // 128
FEATURES = 32
PACKED_ROWS = 32
WANTED_ROW = 22
COEF_ROW = 24
GROUP = 8
VMEM_LIMIT = 16 * 1024 * 1024
CORES = 2
RING = 16
PLANES = 16
FIRST_Z = 12
FIRST_PLANE = 10

smooth_sq = 0.01
four_pi = 4.0 * math.pi
highest = lax.Precision.HIGHEST
f32 = jnp.float32
bf16 = jnp.bfloat16

SMEM = pl.BlockSpec(memory_space=pltpu.SMEM)
VMEM = pl.BlockSpec(memory_space=pltpu.VMEM)


def dot(lhs, rhs, lhs_dim=1, rhs_dim=0):
    return lax.dot_general(
        lhs,
        rhs,
        (((lhs_dim,), (rhs_dim,)), ((), ())),
        precision=highest,
        preferred_element_type=f32,
    )


def even_odd(ref, index):
    even = ref[index, pl.ds(0, HALF, stride=2), :]
    odd = ref[index, pl.ds(1, HALF, stride=2), :]
    return jnp.concatenate([even[:, :RHS], odd[:, :RHS]], axis=1)


def pack(split):
    return jnp.concatenate([split[8 * g : 8 * g + 8] for g in range(4)], axis=1)


def unpack(tile):
    return jnp.concatenate([tile[:, 32 * g : 32 * g + 32] for g in range(4)], axis=0)


def fold(product):
    return product[:RANK, :RHS] + product[RANK:, RHS:]


def dot_parts(lhs, rhs, lhs_dim=1, rhs_dim=0):
    lhs_high, lhs_low = two_parts(lhs)
    rhs_high, rhs_low = two_parts(rhs)
    return lax.dot_general(
        jnp.concatenate([lhs_high, lhs_high, lhs_low], axis=lhs_dim),
        jnp.concatenate([rhs_high, rhs_low, rhs_high], axis=rhs_dim),
        (((lhs_dim,), (rhs_dim,)), ((), ())),
        preferred_element_type=f32,
    )


def up_kernel(dens, col_basis, up_leaf, up_mid, top_out, coefs, leaf_rows, mid_rows, leaf_t, mid_t):
    for chunk in range(CHUNKS):
        lanes = slice(128 * chunk, 128 * chunk + 128)
        leaf_rows[8 * chunk : 8 * chunk + LEAF_DEV, :] = up_leaf[:, lanes]
        mid_rows[8 * chunk : 8 * chunk + MID_DEV, :] = up_mid[:, lanes]
    for c in range(LEAF_DEV):
        cols = slice(LEAF * c, LEAF * c + LEAF)
        leaf_t[c, :, 0:RHS] = dot_parts(col_basis[:, cols], dens[:, cols], 1, 1)
    leaf_split = [even_odd(leaf_t, c) for c in range(LEAF_DEV)]
    for c in range(LEAF_DEV):
        coefs[:, 128 * c : 128 * c + 128] = pack(leaf_split[c])
    for m in range(MID_DEV):
        pair = (2 * m, 2 * m + 1)
        lhs = jnp.concatenate([leaf_rows[pl.ds(c, CHUNKS, stride=8), :] for c in pair], axis=0)
        rhs = jnp.concatenate([leaf_split[c] for c in pair], axis=0)
        mid_t[m, :, 0:RHS] = fold(dot_parts(lhs, rhs, 0, 0))
    mid_split = [even_odd(mid_t, m) for m in range(MID_DEV)]
    for m in range(MID_DEV):
        coefs[:, 128 * (LEAF_DEV + m) : 128 * (LEAF_DEV + m) + 128] = pack(mid_split[m])
    lhs = jnp.concatenate([mid_rows[pl.ds(m, CHUNKS, stride=8), :] for m in range(MID_DEV)], axis=0)
    rhs = jnp.concatenate(mid_split, axis=0)
    leaf_t[0, :, 0:RHS] = fold(dot_parts(lhs, rhs, 0, 0))
    tile = pack(even_odd(leaf_t, 0))
    for peer in range(top_out.shape[0]):
        top_out[peer] = tile


def pack_kernel(dens, points, normals, coefs, adm_top, packed):
    packed[0:RHS, :] = dens[...]
    packed[RHS : RHS + 3, :] = points[...]
    packed[RHS + 3 : RHS + 6, :] = normals[...]
    packed[WANTED_ROW:COEF_ROW, :] = jnp.zeros((COEF_ROW - WANTED_ROW, SPAN), f32)
    packed[WANTED_ROW : WANTED_ROW + 1, 0:ADM_TOP] = adm_top[...].astype(f32)
    packed[COEF_ROW:, 0 : 6 * 128] = coefs[...]
    packed[COEF_ROW:, 6 * 128 :] = jnp.zeros((8, SPAN - 6 * 128), f32)


def pack_call(*operands):
    return pl.pallas_call(
        pack_kernel,
        name="packed_for_neighbours",
        out_shape=jax.ShapeDtypeStruct((PACKED_ROWS, SPAN), f32),
        in_specs=[VMEM] * 5,
        out_specs=VMEM,
        compiler_params=pltpu.CompilerParams(vmem_limit_bytes=VMEM_LIMIT),
        cost_estimate=pl.CostEstimate(flops=100_000_000, bytes_accessed=400_000, transcendentals=0),
    )(*operands)


def up_call(dens, col_basis, up_leaf, up_mid, peers):
    return pl.pallas_call(
        up_kernel,
        name="up_sweep",
        out_shape=(
            jax.ShapeDtypeStruct((peers, 8, 128), f32),
            jax.ShapeDtypeStruct((8, 6 * 128), f32),
        ),
        in_specs=[VMEM] * 4,
        out_specs=(VMEM, VMEM),
        scratch_shapes=[
            pltpu.VMEM((8 * CHUNKS, 128), f32),
            pltpu.VMEM((8 * CHUNKS, 128), f32),
            pltpu.VMEM((LEAF_DEV, RANK, 128), f32),
            pltpu.VMEM((MID_DEV, RANK, 128), f32),
        ],
        cost_estimate=pl.CostEstimate(flops=10_000_000, bytes_accessed=800_000, transcendentals=0),
    )(dens, col_basis, up_leaf, up_mid)


def two_parts(values):
    first = values.astype(bf16)
    return first, (values - first.astype(f32)).astype(bf16)


def bf16_dot(lhs, rhs):
    return lax.dot_general(lhs, rhs, (((1,), (0,)), ((), ())), preferred_element_type=f32)


def three_parts(values):
    first = values.astype(bf16).astype(f32)
    rest = values - first
    second = rest.astype(bf16).astype(f32)
    return first, second, (rest - second).astype(bf16).astype(f32)


def ring_place(z):
    ahead = (z + RING - FIRST_Z) % RING
    return jnp.where(ahead <= RING // 2, jnp.maximum(2 * ahead - 1, 0), 2 * (RING - ahead))


def near_kernel(
    near_list,
    near_count,
    adm_leaf,
    adm_mid,
    own,
    same_chip,
    next_chip,
    couple_leaf,
    couple_mid,
    leaf_mats,
    row_basis,
    adm_top,
    wanted,
    base,
    plan,
    near_out,
    near_t,
    leaf_couple,
    mid_couple,
    feats,
    sources,
    targets,
    dens_parts,
    split_leaf,
    split_mid,
    rows,
    work,
):
    halo = (same_chip, own, next_chip)
    first_leaf = near_list[0, 0]
    first_mid = first_leaf // 2
    core = (first_leaf // LEAF_DEV) % 2

    def held(place, number):
        side = place // number
        return jnp.where(core == 0, place + (2 - 2 * side) * number, place)

    for row, tops in ((0, adm_top), (2, wanted)):
        for a in range(ADM_TOP):
            plane = tops[0, a] // (CORES * RING)
            z = tops[0, a] // CORES % RING
            plan[row, a] = (plane + PLANES - FIRST_PLANE) % PLANES * RING + ring_place(z)
            plan[row + 1, a] = (tops[0, a] % CORES == core).astype(jnp.int32)

    count = jnp.int32(0)
    for i in range(LEAF_DEV):
        limit = near_count[i]
        slots = [near_list[i, j] for j in range(NEAR)]
        used = [jnp.int32(j) < limit for j in range(NEAR)]
        for j in range(NEAR):
            uses = jnp.int32(0)
            fresh = used[j]
            for other in range(NEAR):
                same = jnp.logical_and(used[other], slots[other] == slots[j])
                uses = uses + same.astype(jnp.int32)
                if other < j:
                    fresh = jnp.logical_and(fresh, jnp.logical_not(same))
            work[0, count] = jnp.int32(i)
            work[1, count] = held(slots[j] - first_leaf + LEAF_DEV, LEAF_DEV)
            work[2, count] = uses
            count = count + fresh.astype(jnp.int32)
    for extra in range(GROUP):
        work[0, count + extra] = jnp.int32(0)
        work[1, count + extra] = jnp.int32(0)
        work[2, count + extra] = jnp.int32(0)

    for side in range(3):
        block = halo[side]
        place = block[RHS : RHS + 3, :] - 0.5
        normal = block[RHS + 3 : RHS + 6, :] * (1.0 / four_pi)
        p1, p2, p3 = three_parts(place)
        n1, n2, n3 = three_parts(normal)
        square = jnp.sum(place * place, axis=0, keepdims=True)
        inner = -jnp.sum(place * normal, axis=0, keepdims=True)
        ones = jnp.ones((3, SPAN), f32)
        zeros = jnp.zeros((8, SPAN), f32)
        s1, s2, s3 = three_parts(square)
        i1, i2, i3 = three_parts(inner)
        feats[0:1], feats[1:2], feats[2:3] = s1, s2, s3
        feats[3:6] = ones
        for slot, part in enumerate((p1, p1, p2, p2, p1, p3)):
            feats[6 + 3 * slot : 9 + 3 * slot] = part * -2.0
        feats[24:32] = zeros
        feats[32:40] = zeros
        feats[32:33], feats[33:34], feats[34:35] = i1, i2, i3
        for slot, part in enumerate((n1, n1, n2, n2, n1, n3)):
            feats[38 + 3 * slot : 41 + 3 * slot] = part
        feats[56:64] = zeros
        for leaf in range(LEAF_DEV):
            cols = slice(LEAF * leaf, LEAF * leaf + LEAF)
            place_held = LEAF_DEV * side + leaf
            sources[place_held, :, 0:LEAF] = feats[0:FEATURES, cols].astype(bf16)
            sources[place_held, :, LEAF:] = feats[FEATURES:, cols].astype(bf16)
            dens_high, dens_low = two_parts(block[0:RHS, cols])
            dens_parts[place_held, 0:RHS, 0:LEAF] = dens_high
            dens_parts[place_held, 0:RHS, LEAF:] = dens_high
            dens_parts[place_held, RHS:, 0:LEAF] = dens_low
            dens_parts[place_held, RHS:, LEAF:] = jnp.zeros((RHS, LEAF), bf16)
        if side == 1:
            t1, t2, t3 = three_parts(square + smooth_sq)
            feats[0:3] = ones
            feats[3:4], feats[4:5], feats[5:6] = t1, t2, t3
            for slot, part in enumerate((p1, p2, p1, p2, p3, p1)):
                feats[6 + 3 * slot : 9 + 3 * slot] = part
            feats[24:32] = zeros
            for leaf in range(LEAF_DEV):
                targets[leaf] = jnp.transpose(feats[0:FEATURES, LEAF * leaf : LEAF * leaf + LEAF]).astype(bf16)

    near_t[...] = jnp.zeros((LEAF_DEV, LEAF, 2 * RHS), f32)

    def one_block(entry):
        leaf = work[0, entry]
        source = work[1, entry]
        uses = work[2, entry].astype(f32)
        both = bf16_dot(targets[leaf], sources[source])
        inverse = lax.rsqrt(both[:, :LEAF])
        block = both[:, LEAF:] * (inverse * inverse * inverse)
        high, low = two_parts(block)
        term = lax.dot_general(
            jnp.concatenate([high, low], axis=1),
            dens_parts[source],
            (((1,), (1,)), ((), ())),
            preferred_element_type=f32,
        )
        return leaf, uses * term

    def blocks_from(first, size):
        results = [one_block(first + k) for k in range(size)]
        for leaf, term in results:
            near_t[leaf] = near_t[leaf] + term

    def many_blocks(step, carry):
        blocks_from(2 * GROUP * step, 2 * GROUP)
        return carry

    def some_blocks(step, carry):
        blocks_from(GROUP * step, GROUP)
        return carry

    groups = (count + GROUP - 1) // GROUP
    lax.fori_loop(0, groups // 2, many_blocks, 0)
    lax.fori_loop(groups // 2 * 2, groups, some_blocks, 0)
    for leaf in range(LEAF_DEV):
        total = jnp.transpose(near_t[leaf])
        near_out[leaf] = 0.5 * own[0:RHS, LEAF * leaf : LEAF * leaf + LEAF] + total[:RHS] + total[RHS:]

    for side in range(3):
        for c in range(LEAF_DEV):
            split_leaf[LEAF_DEV * side + c] = unpack(halo[side][COEF_ROW:, 128 * c : 128 * c + 128])
        for m in range(MID_DEV):
            lanes = slice(128 * (LEAF_DEV + m), 128 * (LEAF_DEV + m) + 128)
            split_mid[MID_DEV * side + m] = unpack(halo[side][COEF_ROW:, lanes])
    for couple, number, adm, split, offset, result in (
        (couple_leaf, LEAF_DEV, adm_leaf, split_leaf, first_leaf, leaf_couple),
        (couple_mid, MID_DEV, adm_mid, split_mid, first_mid, mid_couple),
    ):
        slots = couple.shape[0]
        for a in range(slots):
            for chunk in range(CHUNKS):
                rows[a, 8 * chunk : 8 * chunk + number, :] = couple[a, :, 128 * chunk : 128 * chunk + 128]
        for t in range(number):
            lhs = jnp.concatenate([rows[a, pl.ds(t, CHUNKS, stride=8), :] for a in range(slots)], axis=0)
            rhs = jnp.concatenate([split[held(adm[t, a] - offset + number, number)] for a in range(slots)], axis=0)
            result[t] = fold(dot(lhs, rhs, 0, 0))
    for c in range(LEAF_DEV):
        cols = slice(LEAF * c, LEAF * c + LEAF)
        field = leaf_couple[c] + dot(leaf_mats[c], mid_couple[c // 2])
        base[:, cols] = near_out[c] + dot(field, row_basis[:, cols], 0, 0)


def matrix_kernel(couple_top, down_mid, down_leaf, row_basis, top_mats, leaf_mats, top_to_points, mid_mats, rows, natural):
    for chunk in range(CHUNKS):
        rows[16 * chunk : 16 * chunk + ADM_TOP, :] = couple_top[0, :, 128 * chunk : 128 * chunk + 128]
    for group in range(4):
        stack = jnp.concatenate(
            [rows[pl.ds(4 * group + a, CHUNKS, stride=16), :] for a in range(4)], axis=0
        )
        high, low = two_parts(jnp.transpose(stack))
        top_mats[0:128, 128 * group : 128 * group + 128] = high
        top_mats[128:, 128 * group : 128 * group + 128] = low
    for source, result, number in ((down_mid, mid_mats, MID_DEV), (down_leaf, leaf_mats, LEAF_DEV)):
        for chunk in range(CHUNKS):
            rows[8 * chunk : 8 * chunk + number, :] = source[:, 128 * chunk : 128 * chunk + 128]
        for c in range(number):
            wide = rows[pl.ds(c, CHUNKS, stride=8), :]
            swapped = jnp.concatenate([wide[:, RANK:], wide[:, :RANK]], axis=1)
            natural[pl.ds(0, HALF, stride=2), :] = wide
            natural[pl.ds(1, HALF, stride=2), :] = swapped
            result[c] = jnp.transpose(natural[...])[:RANK]
    for c in range(LEAF_DEV):
        cols = slice(LEAF * c, LEAF * c + LEAF)
        high, low = two_parts(dot(dot(leaf_mats[c], mid_mats[c // 2]), row_basis[:, cols], 0, 0))
        top_to_points[0:RANK, cols] = high
        top_to_points[RANK : 2 * RANK, cols] = high
        top_to_points[2 * RANK :, cols] = low


def matrix_call(*operands):
    return pl.pallas_call(
        matrix_kernel,
        name="transposed_matrices",
        out_shape=(
            jax.ShapeDtypeStruct((256, ADM_TOP * HALF), bf16),
            jax.ShapeDtypeStruct((LEAF_DEV, RANK, RANK), f32),
            jax.ShapeDtypeStruct((3 * RANK, SPAN), bf16),
        ),
        in_specs=[VMEM] * 4,
        out_specs=(VMEM,) * 3,
        scratch_shapes=[
            pltpu.VMEM((MID_DEV, RANK, RANK), f32),
            pltpu.VMEM((16 * CHUNKS, 128), f32),
            pltpu.VMEM((RANK, 128), f32),
        ],
        compiler_params=pltpu.CompilerParams(vmem_limit_bytes=VMEM_LIMIT),
        cost_estimate=pl.CostEstimate(flops=2_000_000_000, bytes_accessed=2_000_000, transcendentals=0),
    )(*operands)


def near_call(near_list, near_count, adm_leaf, adm_mid, *rest):
    return pl.pallas_call(
        near_kernel,
        name="near_and_couplings",
        out_shape=(
            jax.ShapeDtypeStruct((RHS, SPAN), f32),
            jax.ShapeDtypeStruct((4, ADM_TOP), jnp.int32),
        ),
        in_specs=[SMEM] * 4 + [VMEM] * 7 + [SMEM] * 2,
        out_specs=(VMEM, SMEM),
        scratch_shapes=[
            pltpu.VMEM((LEAF_DEV, RHS, LEAF), f32),
            pltpu.VMEM((LEAF_DEV, LEAF, 2 * RHS), f32),
            pltpu.VMEM((LEAF_DEV, RANK, RHS), f32),
            pltpu.VMEM((MID_DEV, RANK, RHS), f32),
            pltpu.VMEM((2 * FEATURES, SPAN), f32),
            pltpu.VMEM((3 * LEAF_DEV, FEATURES, 2 * LEAF), bf16),
            pltpu.VMEM((LEAF_DEV, LEAF, FEATURES), bf16),
            pltpu.VMEM((3 * LEAF_DEV, 2 * RHS, 2 * LEAF), bf16),
            pltpu.VMEM((3 * LEAF_DEV, HALF, HALF), f32),
            pltpu.VMEM((3 * MID_DEV, HALF, HALF), f32),
            pltpu.VMEM((ADM_LEAF, 8 * CHUNKS, 128), f32),
            pltpu.SMEM((3, LEAF_DEV * NEAR + 8), jnp.int32),
        ],
        compiler_params=pltpu.CompilerParams(vmem_limit_bytes=VMEM_LIMIT),
        cost_estimate=pl.CostEstimate(flops=4_000_000_000, bytes_accessed=2_000_000, transcendentals=2_000_000),
    )(near_list, near_count, adm_leaf, adm_mid, *rest)


def top_share(top_mats, chosen):
    high, low = two_parts(chosen)
    product = bf16_dot(top_mats[...], jnp.concatenate([high, low], axis=1))
    width = 2 * RHS
    return fold(product[:128, :width] + product[:128, width:] + product[128:, :width])


def held_tops(plan, row, tops):
    return [
        jnp.where(plan[row + 1, a] == 1, tops[plan[row, a]], jnp.zeros((8, 128), f32)) for a in range(ADM_TOP)
    ]


def answer_kernel(plan, own_tops, out):
    for a, tile in enumerate(held_tops(plan, 2, own_tops)):
        out[a] = tile


def answer_call(plan, own_tops):
    return pl.pallas_call(
        answer_kernel,
        name="answer",
        out_shape=jax.ShapeDtypeStruct((ADM_TOP, 8, 128), f32),
        in_specs=[SMEM, VMEM],
        out_specs=VMEM,
        compiler_params=pltpu.CompilerParams(vmem_limit_bytes=VMEM_LIMIT),
        cost_estimate=pl.CostEstimate(flops=1_000_000, bytes_accessed=100_000, transcendentals=0),
    )(plan, own_tops)


def own_kernel(plan, own_tops, top_mats, out):
    out[...] = top_share(top_mats, jnp.concatenate([unpack(tile) for tile in held_tops(plan, 0, own_tops)], axis=0))


def own_call(plan, own_tops, top_mats):
    return pl.pallas_call(
        own_kernel,
        name="own_tops",
        out_shape=jax.ShapeDtypeStruct((RANK, RHS), f32),
        in_specs=[SMEM, VMEM, VMEM],
        out_specs=VMEM,
        compiler_params=pltpu.CompilerParams(vmem_limit_bytes=VMEM_LIMIT),
        cost_estimate=pl.CostEstimate(flops=400_000_000, bytes_accessed=400_000, transcendentals=0),
    )(plan, own_tops, top_mats)


def down_kernel(received, own_share, base, top_mats, top_to_points, out):
    chosen = jnp.concatenate([unpack(received[a]) for a in range(ADM_TOP)], axis=0)
    top_field = own_share[...] + top_share(top_mats, chosen)
    high, low = two_parts(jnp.transpose(top_field))
    out[...] = base[...] + bf16_dot(jnp.concatenate([high, low, high], axis=1), top_to_points[...])


def down_call(*operands):
    return pl.pallas_call(
        down_kernel,
        name="down_sweep",
        out_shape=jax.ShapeDtypeStruct((RHS, SPAN), f32),
        in_specs=[VMEM] * 5,
        out_specs=VMEM,
        compiler_params=pltpu.CompilerParams(vmem_limit_bytes=VMEM_LIMIT),
        cost_estimate=pl.CostEstimate(flops=10_000_000, bytes_accessed=800_000, transcendentals=0),
    )(*operands)


def solution(mesh):
    devices = mesh.devices.size
    ring = [(FIRST_Z + ((i + 1) // 2 if i % 2 else -(i // 2))) % RING for i in range(RING)]
    planes = [(FIRST_PLANE + i) % PLANES for i in range(PLANES)]
    along_z = [[(p * RING + z) * CORES + c for z in ring] for p in range(PLANES) for c in range(CORES)]
    across = [[(p * RING + z) * CORES + c for p in planes] for z in range(RING) for c in range(CORES)]

    def on_device(
        densities,
        points,
        area_normals,
        col_basis,
        row_basis,
        up_leaf,
        up_mid,
        down_leaf,
        down_mid,
        couple_leaf,
        couple_mid,
        couple_top,
        near_list,
        near_count,
        adm_leaf,
        adm_mid,
        adm_top,
    ):
        own_top, coefs = up_call(densities, col_basis, up_leaf, up_mid, RING)
        own_top, coefs, couple_top, down_mid, down_leaf = lax.optimization_barrier(
            (own_top, coefs, couple_top, down_mid, down_leaf)
        )
        packed = pack_call(densities, points, area_normals, coefs, adm_top)
        ring_tops = lax.all_to_all(own_top, "leaf", 0, 0, axis_index_groups=along_z, tiled=True)
        same_chip = lax.ppermute(packed, "leaf", [(i, i ^ 1) for i in range(devices)])
        next_chip = lax.ppermute(packed, "leaf", [(i, ((i + 1) ^ 1) - 1) for i in range(1, devices - 1)])
        top_mats, leaf_mats, top_to_points = matrix_call(couple_top, down_mid, down_leaf, row_basis)
        ring_tops, same_chip, next_chip, top_mats, leaf_mats, top_to_points = lax.optimization_barrier(
            (ring_tops, same_chip, next_chip, top_mats, leaf_mats, top_to_points)
        )
        spread = jnp.broadcast_to(ring_tops.reshape(1, RING * 8, 128), (PLANES, RING * 8, 128))
        core_tops = lax.all_to_all(spread, "leaf", 0, 0, axis_index_groups=across, tiled=True)
        wanted = same_chip[WANTED_ROW : WANTED_ROW + 1, 0:ADM_TOP].astype(jnp.int32)
        base, plan = near_call(
            near_list,
            near_count,
            adm_leaf,
            adm_mid,
            packed,
            same_chip,
            next_chip,
            jnp.swapaxes(couple_leaf, 0, 1),
            jnp.swapaxes(couple_mid, 0, 1),
            leaf_mats,
            row_basis,
            adm_top,
            wanted,
        )
        core_tops, base, plan = lax.optimization_barrier((core_tops, base, plan))
        core_tops = core_tops.reshape(PLANES * RING, 8, 128)
        answers = answer_call(plan, core_tops)
        received = lax.ppermute(answers, "leaf", [(i, i ^ 1) for i in range(devices)])
        answers, plan, core_tops = lax.optimization_barrier((answers, plan, core_tops))
        own_share = own_call(plan, core_tops, top_mats)
        return down_call(
            received,
            own_share,
            base,
            top_mats,
            top_to_points,
        )

    split_last = P(None, "leaf")
    split_first = P("leaf", None)
    split_three = P("leaf", None, None)
    return jax.shard_map(
        on_device,
        mesh=mesh,
        in_specs=(split_last,) * 5
        + (split_first,) * 4
        + (split_three,) * 3
        + (split_first, P("leaf"), split_first, split_first, split_first),
        out_specs=split_last,
        check_vma=False,
    )
```
